32 devices in a mesh: ctx: 4 (over y, x), ch: 8 (over z, core).
Axes of the slice: x: 2, y: 2, z: 4, core: 2. Of those that a mesh axis runs over, the one named last changes fastest.
Arguments:
- streams_in: bfloat16 [3, 4096, 8192], P(None, 'ctx', 'ch'), may hold values from -6 to 6
- out_grad: bfloat16 [4096, 8192], P('ctx', 'ch'), may hold values from -6 to 6
- decay_rate: float32 [8192, 16], P('ch'), may hold values from 2.4414063e-05 to 0.03
- residue: float32 [8192, 16], P('ch'), may hold values from -1.5 to 1.5
- short_filter: float32 [3, 512, 3], replicated, may hold values from -2.5 to 2.5
Outputs:
- layer_out: bfloat16 [4096, 8192], P('ctx', 'ch')
- streams_grad: bfloat16 [3, 4096, 8192], P(None, ('ctx', 'ch'))
The draws below stay inside these ranges and needn't reach their ends.
All inputs are finite; a program needn't handle non-finite values.
Results may differ from the reference program's by a relative error of at most 0.014.
Values may be sent and summed in bfloat16 or wider, within the bound.
A program may use at most 192 MiB of HBM per device.

```python
import math
import jax
import jax.numpy as jnp
from jax import lax

D = 8192
GROUP_SIZE = 16
ORDER = 16
TAPS = 3
BLOCK = 128
GROUPS = 512
TOKENS = 4096


def level_of(key, shape, split, smallest, high):
    factor_of, own = 1.0, jax.random.fold_in(key, 6)
    for dim, shards_of in split:
        steps = jnp.exp(jax.random.uniform(jax.random.fold_in(own, dim), (shards_of,), jnp.float32, smallest / len(split), high / len(split)))
        factor_of = factor_of * jnp.repeat(steps, shape[dim] // shards_of).reshape([-1 if axis == dim else 1 for axis in range(len(shape))])
    return factor_of


def gaussian(stream_key, shape, deviation, limit, cuts=(), held_as=jnp.bfloat16):
    result = jax.random.normal(stream_key, shape, jnp.float32) * deviation
    if len(cuts) > 0:
        result = level_of(stream_key, shape, cuts, -0.22, 0.18) * result
    return jnp.clip(result, min=-limit, max=limit).astype(held_as)


def setup_inputs(seed: int = 0) -> dict:
    key_of = jax.random.split(jax.random.key(seed), 6)
    streams_in = gaussian(key_of[0], (3, TOKENS, D), 1.0, 6.0, ((1, 4), (2, 8)))
    out_grad = gaussian(key_of[1], (TOKENS, D), 1.0, 6.0, ((0, 4), (1, 8)))
    decay_rate = jnp.clip(jnp.exp(math.log(0.03) - 7.1137933 * jax.random.uniform(key_of[2], (D, ORDER), jnp.float32) ** level_of(key_of[2], (D, ORDER), ((0, 8),), -0.2, 0.2)), 2.441406286379788e-05, 0.03)
    residue = gaussian(key_of[3], (D, ORDER), ORDER ** -0.5, 1.5, ((0, 8),), jnp.float32)
    short_filter = gaussian(key_of[4], (3, GROUPS, TAPS), 0.6, 2.5, (), jnp.float32)
    return dict(streams_in=streams_in, out_grad=out_grad, decay_rate=decay_rate, residue=residue, short_filter=short_filter)


highest = lax.Precision.HIGHEST

def filter_tables(decay_rate, residue):
    weight_amp = residue * jnp.sqrt(2.0 * decay_rate)
    lag_index = jnp.arange(BLOCK).astype(decay_rate.dtype)
    powers = jnp.exp(-decay_rate[:, None, :] * lag_index[None, :, None])
    filter_lags = lax.optimization_barrier(jnp.sum(weight_amp[:, None, :] * powers, axis=2))
    offsets = jnp.arange(BLOCK)[:, None] - jnp.arange(BLOCK)[None, :]
    toeplitz = jnp.where(offsets[None] >= 0, filter_lags[:, jnp.maximum(offsets, 0)], 0.0).astype(jnp.bfloat16)
    one_step = jnp.exp(-decay_rate)[:, None, :]
    emit_forward = powers[:, ::-1, :]
    emit_backward = powers
    inject_forward = weight_amp[:, None, :] * powers * one_step
    inject_backward = weight_amp[:, None, :] * powers[:, ::-1, :] * one_step
    block_decay = jnp.exp(-decay_rate * BLOCK)
    return (toeplitz, emit_forward, emit_backward, inject_forward, inject_backward, block_decay)

def short_forward(padded, filters, length):
    summed = [filters[:, None, :, shift_index] * padded[:, TAPS - 1 - shift_index:TAPS - 1 - shift_index + length, :].astype(jnp.float32) for shift_index in range(TAPS)]
    return sum(summed[1:], summed[0])

def short_backward(padded, filters, length):
    summed = [filters[:, None, :, shift_index] * padded[:, shift_index:shift_index + length, :].astype(jnp.float32) for shift_index in range(TAPS)]
    return sum(summed[1:], summed[0])

def channel_block(streams, out_grad, decay_rate, residue, filters):
    length = streams.shape[1]
    chan_count = streams.shape[2]
    block_count = length // BLOCK
    toeplitz, emit_forward, emit_backward, inject_forward, inject_backward, block_decay = filter_tables(decay_rate, residue)
    prior_rows = jnp.zeros((3, TAPS - 1, chan_count), jnp.bfloat16)
    features = short_forward(jnp.concatenate([prior_rows, streams], axis=1), filters, length).astype(jnp.bfloat16)
    query_part = features[0].astype(jnp.float32)
    key_part = features[1].astype(jnp.float32)
    value_part = features[2].astype(jnp.float32)
    product = (key_part * value_part).astype(jnp.bfloat16)
    blocks = product.reshape(block_count, BLOCK, chan_count).astype(jnp.float32)
    toeplitz_wide = toeplitz.astype(jnp.float32)
    inside = jnp.einsum('cij,kjc->kic', toeplitz_wide, blocks, precision=highest)
    emitted = jnp.einsum('kjc,cjn->kcn', blocks, emit_forward, precision=highest)

    def carry_step(state, item):
        return (block_decay * state + item, state)
    zero_state = jnp.zeros((chan_count, ORDER), jnp.float32)
    _, state_before = lax.scan(carry_step, zero_state, emitted)
    long_out = (inside + jnp.einsum('cin,kcn->kic', inject_forward, state_before, precision=highest)).reshape(length, chan_count)
    layer_out = (query_part * long_out).astype(jnp.bfloat16)
    out_wide = out_grad.astype(jnp.float32)
    adjoint = (out_wide * query_part).astype(jnp.bfloat16)
    adj_blocks = adjoint.reshape(block_count, BLOCK, chan_count).astype(jnp.float32)
    inside_back = jnp.einsum('cij,kic->kjc', toeplitz_wide, adj_blocks, precision=highest)
    emitted_back = jnp.einsum('kic,cin->kcn', adj_blocks, emit_backward, precision=highest)
    _, state_after = lax.scan(carry_step, zero_state, emitted_back, reverse=True)
    long_grad = (inside_back + jnp.einsum('cjn,kcn->kjc', inject_backward, state_after, precision=highest)).reshape(length, chan_count)
    stream_grads = jnp.stack([out_wide * long_out, long_grad * value_part, long_grad * key_part]).astype(jnp.bfloat16)
    tail_rows = jnp.zeros((3, TAPS - 1, chan_count), jnp.bfloat16)
    streams_grad = short_backward(jnp.concatenate([stream_grads, tail_rows], axis=1), filters, length).astype(jnp.bfloat16)
    return (layer_out, streams_grad)

def reference(streams_in, out_grad, decay_rate, residue, short_filter):
    chan_count = math.gcd(D, 256)
    all_filters = jnp.repeat(short_filter, GROUP_SIZE, axis=1)

    def one_block(block_index, carried):
        first_col = (block_index * chan_count).astype(jnp.int32)
        streams = lax.dynamic_slice_in_dim(streams_in, first_col, chan_count, 2)
        grads_in = lax.dynamic_slice_in_dim(out_grad, first_col, chan_count, 1)
        rates = lax.dynamic_slice_in_dim(decay_rate, first_col, chan_count, 0)
        residues = lax.dynamic_slice_in_dim(residue, first_col, chan_count, 0)
        filters = lax.dynamic_slice_in_dim(all_filters, first_col, chan_count, 1)
        layer_part, grad_part = channel_block(streams, grads_in, rates, residues, filters)
        return (lax.dynamic_update_slice_in_dim(carried[0], layer_part, first_col, 1), lax.dynamic_update_slice_in_dim(carried[1], grad_part, first_col, 2))
    initial = (jnp.zeros((TOKENS, D), jnp.bfloat16), jnp.zeros((3, TOKENS, D), jnp.bfloat16))
    layer_out, streams_grad = lax.fori_loop(0, D // chan_count, one_block, initial)
    return (layer_out, streams_grad)
```

```python
import functools

import jax
import jax.numpy as jnp
from jax import lax
from jax.experimental import pallas as pl
from jax.experimental.pallas import tpu as pltpu
from jax.sharding import PartitionSpec as P

GROUP_SIZE = 16
TAPS = 3
BLOCK = 128
LANES = 128
ROWS = 8
ORDER = 16
STRIDE = 136
UNROLL = 4
MESH = pl.DeviceIdType.MESH
f32 = jnp.float32
bf16 = jnp.bfloat16


def spread(rows):
    return jnp.broadcast_to(rows[:, None, :], (rows.shape[0], ROWS, LANES))


def steps(body, carry, backward=False, count=BLOCK):
    def some(j, carry):
        for u in range(UNROLL):
            i = j * UNROLL + u
            carry = body(count - 1 - i if backward else i, carry)
        return carry

    return lax.fori_loop(0, count // UNROLL, some, carry)


def kernel(
    nctx, nch, groups,
    x_hbm, og_hbm, rate_ref, res_ref, filt_ref,
    lay_hbm, sgrad_hbm,
    xin, ogin, halo, xf, ogf, qt, kt, vt, ot, pt, at, ef, eb,
    st_send, st_recv, sg, nat, bsend, brecv, send, lay,
    in_sem, halo_send, halo_recv, st_ssem, st_rsem, b_ssem, b_rsem,
    out_ssem, out_rsem, own_sem, lay_sem,
):
    span = x_hbm.shape[1]
    chans = x_hbm.shape[2]
    token_rows = span // nch
    c = lax.axis_index("ctx")
    h = lax.axis_index("ch")

    def lanes(g):
        return pl.ds(pl.multiple_of(g * LANES, LANES), LANES)

    def x_copy(g):
        return pltpu.make_async_copy(x_hbm.at[:, :, lanes(g)], xin.at[g], in_sem.at[0, g])

    def og_copy(g):
        return pltpu.make_async_copy(og_hbm.at[:, lanes(g)], ogin.at[g], in_sem.at[1, g])

    def load(g, _):
        x_copy(g).start()
        og_copy(g).start()
        return 0

    lax.fori_loop(0, groups, load, 0)

    barrier = pltpu.get_barrier_semaphore()

    def greet_ch(k, _):
        pl.semaphore_signal(barrier, inc=1, device_id={"ch": lax.rem(h + k, nch)}, device_id_type=MESH)
        return 0

    def greet_ctx(k, _):
        pl.semaphore_signal(barrier, inc=1, device_id={"ctx": lax.rem(c + k, nctx)}, device_id_type=MESH)
        return 0

    lax.fori_loop(1, nctx, greet_ctx, 0)
    lax.fori_loop(1, nch, greet_ch, 0)
    pl.semaphore_wait(barrier, nch + nctx - 2)

    def halo_copy(g, target):
        return pltpu.make_async_remote_copy(
            src_ref=x_hbm.at[:, pl.ds(span - 16, 16), lanes(g)],
            dst_ref=halo.at[g],
            send_sem=halo_send.at[g],
            recv_sem=halo_recv.at[g],
            device_id={"ctx": target},
            device_id_type=MESH,
        )

    @pl.when(c < nctx - 1)
    def _():
        def go(g, _):
            halo_copy(g, c + 1).start()
            return 0

        lax.fori_loop(0, groups, go, 0)

    def state_copy(g, way, peer, slot):
        return pltpu.make_async_remote_copy(
            src_ref=st_send.at[g, way],
            dst_ref=st_recv.at[g, slot],
            send_sem=st_ssem.at[g, peer],
            recv_sem=st_rsem.at[g, slot],
            device_id={"ctx": peer},
            device_id_type=MESH,
        )

    def edge_copy(g, target):
        return pltpu.make_async_remote_copy(
            src_ref=bsend.at[g],
            dst_ref=brecv.at[g],
            send_sem=b_ssem.at[g],
            recv_sem=b_rsem.at[g],
            device_id={"ctx": target},
            device_id_type=MESH,
        )

    def out_copy(g, peer, source):
        first = pl.multiple_of(source * chans + g * LANES, LANES)
        return pltpu.make_async_remote_copy(
            src_ref=send.at[g, :, pl.ds(pl.multiple_of(peer * token_rows, token_rows), token_rows), :],
            dst_ref=sgrad_hbm.at[:, :, pl.ds(first, LANES)],
            send_sem=out_ssem.at[g, peer],
            recv_sem=out_rsem.at[g, source],
            device_id={"ch": peer},
            device_id_type=MESH,
        )

    def own_copy(g):
        first = pl.multiple_of(h * chans + g * LANES, LANES)
        return pltpu.make_async_copy(
            send.at[g, :, pl.ds(pl.multiple_of(h * token_rows, token_rows), token_rows), :],
            sgrad_hbm.at[:, :, pl.ds(first, LANES)],
            own_sem.at[g],
        )

    def lay_copy(g):
        return pltpu.make_async_copy(lay.at[g], lay_hbm.at[:, lanes(g)], lay_sem.at[g])

    sublane = lax.broadcasted_iota(jnp.int32, (ORDER, ROWS, LANES), 1)
    sublane_f = sublane.astype(f32)

    def tap(g, s, p):
        return jnp.broadcast_to(filt_ref[g, pl.ds(s * TAPS + p, 1), :], (ROWS, LANES))

    def first_phase(g):
        slot = lax.rem(g, 2)
        x_copy(g).wait()
        og_copy(g).wait()

        @pl.when(c > 0)
        def _():
            halo_copy(g, c).wait_recv()
            for s in range(3):
                xf[s, BLOCK - 16 : BLOCK, :] = halo[g, s].astype(f32)

        @pl.when(c == 0)
        def _():
            for s in range(3):
                xf[s, BLOCK - 16 : BLOCK, :] = jnp.zeros((16, LANES), f32)

        def widen(k, _):
            come = pl.ds(pl.multiple_of(k * BLOCK, BLOCK), BLOCK)
            for s in range(3):
                xf[s, pl.ds(pl.multiple_of((k + 1) * STRIDE, 8), BLOCK), :] = xin[g, s, come, :].astype(f32)
            ogf[pl.ds(pl.multiple_of(k * STRIDE, 8), BLOCK), :] = ogin[g, come, :].astype(f32)
            return 0

        lax.fori_loop(0, ROWS, widen, 0)

        rate = rate_ref[g]
        decay = spread(jnp.exp(-rate))
        taps = [[tap(g, s, p) for p in range(TAPS)] for s in range(3)]

        def forward(i, carry):
            state, one, two = carry
            now = [xf[s, pl.ds(STRIDE + i, ROWS, stride=STRIDE), :] for s in range(3)]
            q, k, v = [taps[s][0] * now[s] + taps[s][1] * one[s] + taps[s][2] * two[s] for s in range(3)]
            o = ogf[pl.ds(i, ROWS, stride=STRIDE), :]
            product = k * v
            qt[slot, i] = q
            kt[slot, i] = k
            vt[slot, i] = v
            ot[slot, i] = o
            pt[slot, i] = product
            at[slot, i] = o * q
            return (decay * state + product[None], tuple(now), one)

        zero = jnp.zeros((ORDER, ROWS, LANES), f32)
        one = tuple(xf[s, pl.ds(BLOCK - 1, ROWS, stride=STRIDE), :] for s in range(3))
        two = tuple(xf[s, pl.ds(BLOCK - 2, ROWS, stride=STRIDE), :] for s in range(3))
        state, _, _ = steps(forward, (zero, one, two))
        ef[slot] = state

        def back(i, state):
            return decay * state + at[slot, i][None]

        adj_state = steps(back, zero, True)
        eb[slot] = adj_state

        wide = spread(rate) * (-float(BLOCK))
        st_send[g, 0] = jnp.sum(jnp.exp(wide * (ROWS - 1.0 - sublane_f)) * state, axis=1)
        st_send[g, 1] = jnp.sum(jnp.exp(wide * sublane_f) * adj_state, axis=1)

        def later(j, _):
            state_copy(g, 0, j, c).start()
            return 0

        def earlier(j, _):
            state_copy(g, 1, j, c).start()
            return 0

        lax.fori_loop(c + 1, nctx, later, 0)
        lax.fori_loop(0, c, earlier, 0)

    def second_phase(g):
        slot = lax.rem(g, 2)
        rate = rate_ref[g]
        decay = spread(jnp.exp(-rate))
        amp = spread(res_ref[g] * jnp.sqrt(2.0 * rate))
        hop = jnp.exp(-rate * float(span))

        def arrive(j, total):
            state_copy(g, 0, j, j).wait_recv()
            return hop * total + st_recv[g, j]

        def arrive_back(k, total):
            j = nctx - 1 - k
            state_copy(g, 1, j, j).wait_recv()
            return hop * total + st_recv[g, j]

        none = jnp.zeros((ORDER, LANES), f32)
        incoming = lax.fori_loop(0, c, arrive, none)
        outgoing = lax.fori_loop(0, nctx - 1 - c, arrive_back, none)

        def scan(emitted, entry, backward):
            def shift(a, by, fill):
                moved = pltpu.roll(a, ROWS - by if backward else by, 1)
                keep = sublane < ROWS - by if backward else sublane >= by
                return jnp.where(keep, moved, fill)

            total = shift(emitted, 1, spread(entry))
            factor = spread(jnp.exp(-rate * float(BLOCK)))
            for by in (1, 2, 4):
                total = total + factor * shift(total, by, 0.0)
                factor = factor * factor
            return total

        def forward(i, state):
            state = decay * state + pt[slot, i][None]
            long_out = jnp.sum(amp * state, axis=0)
            nat[3, pl.ds(i, ROWS, stride=STRIDE), :] = qt[slot, i] * long_out
            sg[0, i] = ot[slot, i] * long_out
            return state

        steps(forward, scan(ef[slot], incoming, False))

        def back(i, state):
            state = decay * state + at[slot, i][None]
            long_grad = jnp.sum(amp * state, axis=0)
            sg[1, i] = long_grad * vt[slot, i]
            sg[2, i] = long_grad * kt[slot, i]
            return state

        steps(back, scan(eb[slot], outgoing, True), True)

        for s in range(3):
            for r in range(TAPS - 1):
                bsend[g, s, r] = sg[s, r]

        @pl.when(c > 0)
        def _():
            edge_copy(g, c - 1).start()

        taps = [[tap(g, s, p) for p in range(TAPS)] for s in range(3)]

        def short(i, _):
            for s in range(3):
                nat[s, pl.ds(i, ROWS, stride=STRIDE), :] = (
                    taps[s][0] * sg[s, i] + taps[s][1] * sg[s, i + 1] + taps[s][2] * sg[s, i + 2]
                )
            return 0

        steps(short, 0, count=BLOCK - UNROLL)

        def narrow_lay(k, _):
            come = pl.ds(pl.multiple_of(k * STRIDE, 8), BLOCK)
            lay[g, pl.ds(pl.multiple_of(k * BLOCK, BLOCK), BLOCK), :] = nat[3, come, :].astype(bf16)
            return 0

        lax.fori_loop(0, ROWS, narrow_lay, 0)
        lay_copy(g).start()

        @pl.when(c == nctx - 1)
        def _():
            brecv[g] = jnp.zeros((3, TAPS - 1, ROWS, LANES), f32)

        @pl.when(c < nctx - 1)
        def _():
            edge_copy(g, c).wait_recv()

        last = lax.broadcasted_iota(jnp.int32, (ROWS, LANES), 0) == ROWS - 1
        for s in range(3):
            for r in range(TAPS - 1):
                sg[s, BLOCK + r] = jnp.where(
                    last, pltpu.roll(brecv[g, s, r], ROWS - 1, 0), pltpu.roll(sg[s, r], ROWS - 1, 0)
                )
        for i in range(BLOCK - UNROLL, BLOCK):
            short(i, 0)

        def narrow(k, _):
            come = pl.ds(pl.multiple_of(k * STRIDE, 8), BLOCK)
            for s in range(3):
                send[g, s, pl.ds(pl.multiple_of(k * BLOCK, BLOCK), BLOCK), :] = nat[s, come, :].astype(bf16)
            return 0

        lax.fori_loop(0, ROWS, narrow, 0)

        def go(k, _):
            peer = lax.rem(h + lax.rem(k + nch // 2 - 2, nch - 1) + 1, nch)
            out_copy(g, peer, h).start()
            return 0

        lax.fori_loop(1, nch, go, 0)
        own_copy(g).start()

    def both(t, _):
        @pl.when(t < groups)
        def _():
            first_phase(t)

        @pl.when(t > 0)
        def _():
            second_phase(t - 1)

        return 0

    lax.fori_loop(0, groups + 1, both, 0)

    def finish(g, _):
        @pl.when(c < nctx - 1)
        def _():
            halo_copy(g, c).wait_send()

        @pl.when(c > 0)
        def _():
            edge_copy(g, c).wait_send()

        def later(j, _):
            state_copy(g, 0, j, c).wait_send()
            return 0

        def earlier(j, _):
            state_copy(g, 1, j, c).wait_send()
            return 0

        lax.fori_loop(c + 1, nctx, later, 0)
        lax.fori_loop(0, c, earlier, 0)
        lay_copy(g).wait()
        own_copy(g).wait()

        def out(k, _):
            peer = lax.rem(h + k, nch)
            out_copy(g, peer, h).wait_send()
            out_copy(g, peer, peer).wait_recv()
            return 0

        lax.fori_loop(1, nch, out, 0)
        return 0

    lax.fori_loop(0, groups, finish, 0)


def shards(nctx, nch, streams_in, out_grad, decay_rate, residue, short_filter):
    _, span, chans = streams_in.shape
    assert span == ROWS * BLOCK and chans % LANES == 0
    groups = chans // LANES
    token_rows = span // nch
    rate = decay_rate.reshape(groups, LANES, ORDER).swapaxes(1, 2)
    res = residue.reshape(groups, LANES, ORDER).swapaxes(1, 2)
    here = chans // GROUP_SIZE
    local = lax.dynamic_slice_in_dim(short_filter, lax.axis_index("ch") * here, here, 1)
    filt = jnp.repeat(local, GROUP_SIZE, axis=1).reshape(3, groups, LANES, TAPS)
    filt = filt.transpose(1, 0, 3, 2).reshape(groups, 3 * TAPS, LANES)
    turned = (2, BLOCK, ROWS, LANES)
    states = (2, ORDER, ROWS, LANES)
    edge = (groups, 3, TAPS - 1, ROWS, LANES)
    dma = pltpu.SemaphoreType.DMA
    return pl.pallas_call(
        functools.partial(kernel, nctx, nch, groups),
        out_shape=(
            jax.ShapeDtypeStruct((span, chans), bf16),
            jax.ShapeDtypeStruct((3, token_rows, chans * nch), bf16),
        ),
        in_specs=[pl.BlockSpec(memory_space=pl.ANY)] * 2 + [pl.BlockSpec(memory_space=pltpu.VMEM)] * 3,
        out_specs=(pl.BlockSpec(memory_space=pl.ANY),) * 2,
        scratch_shapes=[
            pltpu.VMEM((groups, 3, span, LANES), bf16),
            pltpu.VMEM((groups, span, LANES), bf16),
            pltpu.VMEM((groups, 3, 16, LANES), bf16),
            pltpu.VMEM((3, (ROWS + 1) * STRIDE, LANES), f32),
            pltpu.VMEM((ROWS * STRIDE, LANES), f32),
            *[pltpu.VMEM(turned, f32) for _ in range(6)],
            *[pltpu.VMEM(states, f32) for _ in range(2)],
            pltpu.VMEM((groups, 2, ORDER, LANES), f32),
            pltpu.VMEM((groups, nctx, ORDER, LANES), f32),
            pltpu.VMEM((3, BLOCK + TAPS - 1, ROWS, LANES), f32),
            pltpu.VMEM((4, ROWS * STRIDE, LANES), f32),
            pltpu.VMEM(edge, f32),
            pltpu.VMEM(edge, f32),
            pltpu.VMEM((groups, 3, span, LANES), bf16),
            pltpu.VMEM((groups, span, LANES), bf16),
            dma((2, groups)),
            dma((groups,)),
            dma((groups,)),
            dma((groups, nctx)),
            dma((groups, nctx)),
            dma((groups,)),
            dma((groups,)),
            dma((groups, nch)),
            dma((groups, nch)),
            dma((groups,)),
            dma((groups,)),
        ],
        compiler_params=pltpu.CompilerParams(
            collective_id=0, has_side_effects=True, vmem_limit_bytes=48 * 1024 * 1024
        ),
        cost_estimate=pl.CostEstimate(
            flops=span * chans * 250, bytes_accessed=16 * span * chans, transcendentals=0
        ),
    )(streams_in, out_grad, rate, res, filt)


def solution(mesh):
    return jax.shard_map(
        functools.partial(shards, mesh.shape["ctx"], mesh.shape["ch"]),
        mesh=mesh,
        in_specs=(P(None, "ctx", "ch"), P("ctx", "ch"), P("ch", None), P("ch", None), P()),
        out_specs=(P("ctx", "ch"), P(None, ("ctx", "ch"), None)),
        check_vma=False,
    )
```

```python
import functools

import jax
import jax.numpy as jnp
from jax import lax
from jax.experimental import pallas as pl
from jax.experimental.pallas import tpu as pltpu
from jax.sharding import PartitionSpec as P

GROUP_SIZE = 16
TAPS = 3
BLOCK = 128
LANES = 128
ROWS = 8
ORDER = 16
STRIDE = 136
UNROLL = 4
MESH = pl.DeviceIdType.MESH
PARTS = (pl.ds(0, 1), pl.ds(1, 2))
f32 = jnp.float32
bf16 = jnp.bfloat16


def spread(rows):
    return jnp.broadcast_to(rows[:, None, :], (rows.shape[0], ROWS, LANES))


def steps(body, carry, backward=False, count=BLOCK):
    def some(j, carry):
        for u in range(UNROLL):
            i = j * UNROLL + u
            carry = body(count - 1 - i if backward else i, carry)
        return carry

    return lax.fori_loop(0, count // UNROLL, some, carry)


def kernel(
    nctx, nch, groups,
    x_hbm, og_hbm, rate_ref, res_ref, filt_ref,
    lay, sgrad,
    xin, ogin, halo, xf, ogf, filt, qt, kt, vt, ot, pt, at, ef, eb,
    st_send, st_recv, sg, nat, bsend, brecv, send,
    in_sem, halo_send, halo_recv, st_ssem, st_rsem, b_ssem, b_rsem,
    out_ssem, out_rsem, own_sem,
):
    span = x_hbm.shape[1]
    chans = x_hbm.shape[2]
    token_rows = span // nch
    c = lax.axis_index("ctx")
    h = lax.axis_index("ch")

    def lanes(g):
        return pl.ds(pl.multiple_of(g * LANES, LANES), LANES)

    def x_copy(g):
        return pltpu.make_async_copy(x_hbm.at[:, :, lanes(g)], xin.at[g], in_sem.at[0, g])

    def og_copy(g):
        return pltpu.make_async_copy(og_hbm.at[:, lanes(g)], ogin.at[g], in_sem.at[1, g])

    def load(g, _):
        x_copy(g).start()
        og_copy(g).start()
        return 0

    lax.fori_loop(0, groups, load, 0)

    barrier = pltpu.get_barrier_semaphore()

    def greet_ch(k, _):
        pl.semaphore_signal(barrier, inc=1, device_id={"ch": lax.rem(h + k, nch)}, device_id_type=MESH)
        return 0

    def greet_ctx(k, _):
        pl.semaphore_signal(barrier, inc=1, device_id={"ctx": lax.rem(c + k, nctx)}, device_id_type=MESH)
        return 0

    lax.fori_loop(1, nctx, greet_ctx, 0)
    lax.fori_loop(1, nch, greet_ch, 0)

    for s in range(3):
        xf[s, BLOCK - 16 : BLOCK, :] = jnp.zeros((16, LANES), f32)

    def widen(g):
        x_copy(g).wait()
        og_copy(g).wait()

        def block(k, _):
            come = pl.ds(pl.multiple_of(k * BLOCK, BLOCK), BLOCK)
            for s in range(3):
                xf[s, pl.ds(pl.multiple_of((k + 1) * STRIDE, 8), BLOCK), :] = xin[g, s, come, :].astype(f32)
            ogf[pl.ds(pl.multiple_of(k * STRIDE, 8), BLOCK), :] = ogin[g, come, :].astype(f32)
            return 0

        lax.fori_loop(0, ROWS, block, 0)

    widen(0)
    pl.semaphore_wait(barrier, nch + nctx - 2)

    def halo_copy(g, target):
        return pltpu.make_async_remote_copy(
            src_ref=x_hbm.at[:, pl.ds(span - 16, 16), lanes(g)],
            dst_ref=halo.at[g],
            send_sem=halo_send.at[g],
            recv_sem=halo_recv.at[g],
            device_id={"ctx": target},
            device_id_type=MESH,
        )

    @pl.when(c < nctx - 1)
    def _():
        def go(g, _):
            halo_copy(g, c + 1).start()
            return 0

        lax.fori_loop(0, groups, go, 0)

    def state_copy(g, way, peer, slot):
        return pltpu.make_async_remote_copy(
            src_ref=st_send.at[g, way],
            dst_ref=st_recv.at[g, slot],
            send_sem=st_ssem.at[g, peer],
            recv_sem=st_rsem.at[g, slot],
            device_id={"ctx": peer},
            device_id_type=MESH,
        )

    def edge_copy(g, part, target):
        streams = PARTS[part]
        return pltpu.make_async_remote_copy(
            src_ref=bsend.at[g, streams],
            dst_ref=brecv.at[g, streams],
            send_sem=b_ssem.at[part, g],
            recv_sem=b_rsem.at[part, g],
            device_id={"ctx": target},
            device_id_type=MESH,
        )

    def out_copy(g, part, peer, source):
        streams = PARTS[part]
        first = pl.multiple_of(source * chans + g * LANES, LANES)
        return pltpu.make_async_remote_copy(
            src_ref=send.at[g, streams, pl.ds(pl.multiple_of(peer * token_rows, token_rows), token_rows), :],
            dst_ref=sgrad.at[streams, :, pl.ds(first, LANES)],
            send_sem=out_ssem.at[part, g, peer],
            recv_sem=out_rsem.at[part, g, source],
            device_id={"ch": peer},
            device_id_type=MESH,
        )

    def own_copy(g):
        first = pl.multiple_of(h * chans + g * LANES, LANES)
        return pltpu.make_async_copy(
            send.at[g, :, pl.ds(pl.multiple_of(h * token_rows, token_rows), token_rows), :],
            sgrad.at[:, :, pl.ds(first, LANES)],
            own_sem.at[g],
        )

    sublane = lax.broadcasted_iota(jnp.int32, (ORDER, ROWS, LANES), 1)
    sublane_f = sublane.astype(f32)

    first_row = lax.broadcasted_iota(jnp.int32, (ROWS, LANES), 0) == 0
    last_row = lax.broadcasted_iota(jnp.int32, (ROWS, LANES), 0) == ROWS - 1

    def load_taps(slot):
        return [
            [jnp.broadcast_to(filt[slot, s, p : p + 1, :], (ROWS, LANES)) for p in range(TAPS)] for s in range(3)
        ]

    def first_phase(g):
        slot = lax.rem(g, 2)
        all_groups = filt_ref.shape[2]
        base = h * (chans // GROUP_SIZE) + g * (LANES // GROUP_SIZE)
        of_lane = lax.broadcasted_iota(jnp.int32, (all_groups, LANES), 1) // GROUP_SIZE + base
        pick = (lax.broadcasted_iota(jnp.int32, (all_groups, LANES), 0) == of_lane).astype(f32)
        for s in range(3):
            filt[slot, s, 0:TAPS, :] = jnp.dot(
                filt_ref[s], pick, precision=lax.Precision.HIGHEST, preferred_element_type=f32
            )

        rate = rate_ref[:, lanes(g)]
        decay = spread(jnp.exp(-rate))
        taps = load_taps(slot)

        def forward(i, carry):
            state, one, two = carry
            now = [xf[s, pl.ds(STRIDE + i, ROWS, stride=STRIDE), :] for s in range(3)]
            q, k, v = [taps[s][0] * now[s] + taps[s][1] * one[s] + taps[s][2] * two[s] for s in range(3)]
            o = ogf[pl.ds(i, ROWS, stride=STRIDE), :]
            product = k * v
            qt[slot, i] = q
            kt[slot, i] = k
            vt[slot, i] = v
            ot[slot, i] = o
            pt[slot, i] = product
            at[slot, i] = o * q
            return (decay * state + product[None], tuple(now), one)

        zero = jnp.zeros((ORDER, ROWS, LANES), f32)
        one = tuple(xf[s, pl.ds(BLOCK - 1, ROWS, stride=STRIDE), :] for s in range(3))
        two = tuple(xf[s, pl.ds(BLOCK - 2, ROWS, stride=STRIDE), :] for s in range(3))
        state, _, _ = steps(forward, (zero, one, two))
        ef[slot] = state

        @pl.when(c > 0)
        def _():
            halo_copy(g, c).wait_recv()
            before = [halo[g, s].astype(f32) for s in range(3)]
            for i in range(TAPS - 1):
                more = []
                for s in range(3):
                    term = taps[s][i + 1] * jnp.broadcast_to(before[s][15:16], (ROWS, LANES))
                    if i == 0:
                        term = term + taps[s][2] * jnp.broadcast_to(before[s][14:15], (ROWS, LANES))
                    more.append(jnp.where(first_row, term, 0.0))
                q = qt[slot, i] + more[0]
                k = kt[slot, i] + more[1]
                v = vt[slot, i] + more[2]
                change = k * v - pt[slot, i]
                qt[slot, i] = q
                kt[slot, i] = k
                vt[slot, i] = v
                pt[slot, i] = k * v
                at[slot, i] = ot[slot, i] * q
                ef[slot] += spread(jnp.exp(-rate * float(BLOCK - 1 - i))) * change[None]

        wide = spread(rate) * (-float(BLOCK))
        st_send[g, 0] = jnp.sum(jnp.exp(wide * (ROWS - 1.0 - sublane_f)) * ef[slot], axis=1)

        def later(j, _):
            state_copy(g, 0, j, c).start()
            return 0

        lax.fori_loop(c + 1, nctx, later, 0)

        def back(i, state):
            return decay * state + at[slot, i][None]

        adj_state = steps(back, zero, True)
        eb[slot] = adj_state
        st_send[g, 1] = jnp.sum(jnp.exp(wide * sublane_f) * adj_state, axis=1)

        def earlier(j, _):
            state_copy(g, 1, j, c).start()
            return 0

        lax.fori_loop(0, c, earlier, 0)

    def second_phase(g):
        slot = lax.rem(g, 2)
        rate = rate_ref[:, lanes(g)]
        decay = spread(jnp.exp(-rate))
        amp = spread(res_ref[:, lanes(g)] * jnp.sqrt(2.0 * rate))
        taps = load_taps(slot)
        hop = jnp.exp(-rate * float(span))

        def arrive(j, total):
            state_copy(g, 0, j, j).wait_recv()
            return hop * total + st_recv[g, j]

        def arrive_back(k, total):
            j = nctx - 1 - k
            state_copy(g, 1, j, j).wait_recv()
            return hop * total + st_recv[g, j]

        none = jnp.zeros((ORDER, LANES), f32)
        def scan(emitted, entry, backward):
            def shift(a, by, fill):
                moved = pltpu.roll(a, ROWS - by if backward else by, 1)
                keep = sublane < ROWS - by if backward else sublane >= by
                return jnp.where(keep, moved, fill)

            total = shift(emitted, 1, spread(entry))
            factor = spread(jnp.exp(-rate * float(BLOCK)))
            for by in (1, 2, 4):
                total = total + factor * shift(total, by, 0.0)
                factor = factor * factor
            return total

        def short(s, i):
            nat[s, pl.ds(i, ROWS, stride=STRIDE), :] = (
                taps[s][0] * sg[s, i] + taps[s][1] * sg[s, i + 1] + taps[s][2] * sg[s, i + 2]
            )

        def narrow(s, first, last):
            def block(k, _):
                come = pl.ds(pl.multiple_of(k * STRIDE, 8), BLOCK)
                send[g, s, pl.ds(pl.multiple_of(k * BLOCK, BLOCK), BLOCK), :] = nat[s, come, :].astype(bf16)
                return 0

            lax.fori_loop(first, last, block, 0)

        early = nch * (ROWS - 1) // ROWS

        def finish_part(part):
            streams = PARTS[part]
            for s in range(streams.start, streams.start + streams.size):
                for r in range(TAPS - 1):
                    bsend[g, s, r] = sg[s, r]
                    sg[s, BLOCK + r] = pltpu.roll(sg[s, r], ROWS - 1, 0)

            @pl.when(c > 0)
            def _():
                edge_copy(g, part, c - 1).start()

            def some(i, _):
                for s in range(streams.start, streams.start + streams.size):
                    short(s, i)
                return 0

            steps(some, 0)
            for s in range(streams.start, streams.start + streams.size):
                narrow(s, 0, ROWS - 1)

            def go(k, _):
                peer = lax.rem(h + lax.rem(k + nch // 2 - 2, nch - 1) + 1, nch)

                @pl.when(peer < early)
                def _():
                    out_copy(g, part, peer, h).start()

                return 0

            lax.fori_loop(1, nch, go, 0)

        def forward(i, state):
            state = decay * state + pt[slot, i][None]
            long_out = jnp.sum(amp * state, axis=0)
            nat[3, pl.ds(i, ROWS, stride=STRIDE), :] = qt[slot, i] * long_out
            sg[0, i] = ot[slot, i] * long_out
            return state

        incoming = lax.fori_loop(0, c, arrive, none)
        steps(forward, scan(ef[slot], incoming, False))
        finish_part(0)

        def back(i, state):
            state = decay * state + at[slot, i][None]
            long_grad = jnp.sum(amp * state, axis=0)
            sg[1, i] = long_grad * vt[slot, i]
            sg[2, i] = long_grad * kt[slot, i]
            return state

        outgoing = lax.fori_loop(0, nctx - 1 - c, arrive_back, none)
        steps(back, scan(eb[slot], outgoing, True), True)
        finish_part(1)

        def narrow_lay(k, _):
            come = pl.ds(pl.multiple_of(k * STRIDE, 8), BLOCK)
            lay[pl.ds(pl.multiple_of(k * BLOCK, BLOCK), BLOCK), lanes(g)] = nat[3, come, :].astype(bf16)
            return 0

        lax.fori_loop(0, ROWS, narrow_lay, 0)

        @pl.when(c == nctx - 1)
        def _():
            brecv[g] = jnp.zeros((3, TAPS - 1, ROWS, LANES), f32)

        @pl.when(c < nctx - 1)
        def _():
            edge_copy(g, 0, c).wait_recv()
            edge_copy(g, 1, c).wait_recv()

        for s in range(3):
            for r in range(TAPS - 1):
                sg[s, BLOCK + r] = jnp.where(last_row, pltpu.roll(brecv[g, s, r], ROWS - 1, 0), sg[s, BLOCK + r])
            for i in range(BLOCK - TAPS + 1, BLOCK):
                short(s, i)
            narrow(s, ROWS - 1, ROWS)

        def rest(peer, _):
            @pl.when(peer != h)
            def _():
                out_copy(g, 0, peer, h).start()
                out_copy(g, 1, peer, h).start()

            return 0

        lax.fori_loop(early, nch, rest, 0)
        own_copy(g).start()

    def both(t, _):
        @pl.when(t < groups)
        def _():
            first_phase(t)

        @pl.when(t != 1)
        def _():
            second_phase(jnp.maximum(t - 1, 0))

        @pl.when(t + 1 < groups)
        def _():
            widen(t + 1)

        return 0

    lax.fori_loop(0, groups + 1, both, 0)

    def finish(g, _):
        @pl.when(c < nctx - 1)
        def _():
            halo_copy(g, c).wait_send()

        @pl.when(c > 0)
        def _():
            edge_copy(g, 0, c).wait_send()
            edge_copy(g, 1, c).wait_send()

        def later(j, _):
            state_copy(g, 0, j, c).wait_send()
            return 0

        def earlier(j, _):
            state_copy(g, 1, j, c).wait_send()
            return 0

        lax.fori_loop(c + 1, nctx, later, 0)
        lax.fori_loop(0, c, earlier, 0)
        own_copy(g).wait()

        def out(k, _):
            peer = lax.rem(h + k, nch)
            for part in range(2):
                out_copy(g, part, peer, h).wait_send()
                out_copy(g, part, peer, peer).wait_recv()
            return 0

        lax.fori_loop(1, nch, out, 0)
        return 0

    lax.fori_loop(0, groups, finish, 0)


def place(lay, sgrad, lay_out, sgrad_out, sem):
    copies = [pltpu.make_async_copy(sgrad.at[s], sgrad_out.at[s], sem.at[s]) for s in range(3)]
    copies.append(pltpu.make_async_copy(lay, lay_out, sem.at[3]))
    for copy in copies:
        copy.start()
    for copy in copies:
        copy.wait()


def shards(nctx, nch, streams_in, out_grad, decay_rate, residue, short_filter):
    _, span, chans = streams_in.shape
    assert span == ROWS * BLOCK and chans % LANES == 0
    groups = chans // LANES
    token_rows = span // nch
    rate = decay_rate.T
    res = residue.T
    filt = short_filter.transpose(0, 2, 1)
    turned = (2, BLOCK, ROWS, LANES)
    states = (2, ORDER, ROWS, LANES)
    edge = (groups, 3, TAPS - 1, ROWS, LANES)
    dma = pltpu.SemaphoreType.DMA
    whole = pl.BlockSpec(memory_space=pltpu.VMEM)
    held = pl.pallas_call(
        functools.partial(kernel, nctx, nch, groups),
        out_shape=(
            jax.ShapeDtypeStruct((span, chans), bf16),
            jax.ShapeDtypeStruct((3, token_rows, chans * nch), bf16),
        ),
        in_specs=[pl.BlockSpec(memory_space=pltpu.HBM)] * 2 + [whole] * 3,
        out_specs=(whole, pl.BlockSpec(memory_space=pl.ANY)),
        scratch_shapes=[
            pltpu.VMEM((groups, 3, span, LANES), bf16),
            pltpu.VMEM((groups, span, LANES), bf16),
            pltpu.VMEM((groups, 3, 16, LANES), bf16),
            pltpu.VMEM((3, (ROWS + 1) * STRIDE, LANES), f32),
            pltpu.VMEM((ROWS * STRIDE, LANES), f32),
            pltpu.VMEM((2, 3, 8, LANES), f32),
            *[pltpu.VMEM(turned, f32) for _ in range(6)],
            *[pltpu.VMEM(states, f32) for _ in range(2)],
            pltpu.VMEM((groups, 2, ORDER, LANES), f32),
            pltpu.VMEM((groups, nctx, ORDER, LANES), f32),
            pltpu.VMEM((3, BLOCK + TAPS - 1, ROWS, LANES), f32),
            pltpu.VMEM((4, ROWS * STRIDE, LANES), f32),
            pltpu.VMEM(edge, f32),
            pltpu.VMEM(edge, f32),
            pltpu.VMEM((groups, 3, span, LANES), bf16),
            dma((2, groups)),
            dma((groups,)),
            dma((groups,)),
            dma((groups, nctx)),
            dma((groups, nctx)),
            dma((2, groups)),
            dma((2, groups)),
            dma((2, groups, nch)),
            dma((2, groups, nch)),
            dma((groups,)),
        ],
        compiler_params=pltpu.CompilerParams(
            collective_id=0, has_side_effects=True, vmem_limit_bytes=40 * 1024 * 1024
        ),
        cost_estimate=pl.CostEstimate(
            flops=span * chans * 250, bytes_accessed=16 * span * chans, transcendentals=0
        ),
    )(streams_in, out_grad, rate, res, filt)
    return pl.pallas_call(
        place,
        out_shape=tuple(jax.ShapeDtypeStruct(a.shape, a.dtype) for a in held),
        in_specs=[pl.BlockSpec(memory_space=pl.ANY)] * 2,
        out_specs=(pl.BlockSpec(memory_space=pl.ANY),) * 2,
        scratch_shapes=[dma((4,))],
        compiler_params=pltpu.CompilerParams(vmem_limit_bytes=16 * 1024 * 1024),
    )(*held)


def solution(mesh):
    return jax.shard_map(
        functools.partial(shards, mesh.shape["ctx"], mesh.shape["ch"]),
        mesh=mesh,
        in_specs=(P(None, "ctx", "ch"), P("ctx", "ch"), P("ch", None), P("ch", None), P()),
        out_specs=(P("ctx", "ch"), P(None, ("ctx", "ch"), None)),
        check_vma=False,
    )
```

```python
import functools

import jax
import jax.numpy as jnp
from jax import lax
from jax.experimental import pallas as pl
from jax.experimental.pallas import tpu as pltpu
from jax.sharding import PartitionSpec as P

GROUP_SIZE = 16
TAPS = 3
BLOCK = 128
LANES = 128
ROWS = 8
ORDER = 16
STRIDE = 136
UNROLL = 4
MESH = pl.DeviceIdType.MESH
PARTS = (pl.ds(0, 1), pl.ds(1, 2))
f32 = jnp.float32
bf16 = jnp.bfloat16


def spread(rows):
    return jnp.broadcast_to(rows[:, None, :], (rows.shape[0], ROWS, LANES))


def steps(body, carry, backward=False, count=BLOCK):
    def some(j, carry):
        for u in range(UNROLL):
            i = j * UNROLL + u
            carry = body(count - 1 - i if backward else i, carry)
        return carry

    return lax.fori_loop(0, count // UNROLL, some, carry)


def kernel(
    nctx, nch, groups,
    x_hbm, og_hbm, rate_ref, res_ref, filt_ref,
    lay, sgrad,
    xin, ogin, halo, xf, ogf, all_taps, filt, qt, kt, vt, ot, pt, at, ef, eb,
    st_send, st_recv, sg, nat, bsend, brecv, send,
    in_sem, halo_send, halo_recv, st_ssem, st_rsem, b_ssem, b_rsem,
    out_ssem, out_rsem, own_sem,
):
    span = x_hbm.shape[1]
    chans = x_hbm.shape[2]
    token_rows = span // nch
    c = lax.axis_index("ctx")
    h = lax.axis_index("ch")

    def lanes(g):
        return pl.ds(pl.multiple_of(g * LANES, LANES), LANES)

    def x_copy(g):
        return pltpu.make_async_copy(x_hbm.at[:, :, lanes(g)], xin.at[g], in_sem.at[0, g])

    def og_copy(g):
        return pltpu.make_async_copy(og_hbm.at[:, lanes(g)], ogin.at[g], in_sem.at[1, g])

    def load(g, _):
        x_copy(g).start()
        og_copy(g).start()
        return 0

    load(0, 0)

    barrier = pltpu.get_barrier_semaphore()

    def greet_ch(k, _):
        pl.semaphore_signal(barrier, inc=1, device_id={"ch": lax.rem(h + k, nch)}, device_id_type=MESH)
        return 0

    def greet_ctx(k, _):
        pl.semaphore_signal(barrier, inc=1, device_id={"ctx": lax.rem(c + k, nctx)}, device_id_type=MESH)
        return 0

    lax.fori_loop(1, nctx, greet_ctx, 0)
    lax.fori_loop(1, nch, greet_ch, 0)

    all_taps[...] = jnp.zeros((16, LANES), f32)
    for s in range(3):
        xf[s, BLOCK - 16 : BLOCK, :] = jnp.zeros((16, LANES), f32)

    def widen(g):
        x_copy(g).wait()
        og_copy(g).wait()

        def block(k, _):
            come = pl.ds(pl.multiple_of(k * BLOCK, BLOCK), BLOCK)
            for s in range(3):
                xf[s, pl.ds(pl.multiple_of((k + 1) * STRIDE, 8), BLOCK), :] = xin[g, s, come, :].astype(f32)
            ogf[pl.ds(pl.multiple_of(k * STRIDE, 8), BLOCK), :] = ogin[g, come, :].astype(f32)
            return 0

        lax.fori_loop(0, ROWS, block, 0)

    widen(0)
    lax.fori_loop(1, groups, load, 0)
    pl.semaphore_wait(barrier, nch + nctx - 2)

    def halo_copy(g, target):
        return pltpu.make_async_remote_copy(
            src_ref=x_hbm.at[:, pl.ds(span - 16, 16), lanes(g)],
            dst_ref=halo.at[g],
            send_sem=halo_send.at[g],
            recv_sem=halo_recv.at[g],
            device_id={"ctx": target},
            device_id_type=MESH,
        )

    @pl.when(c < nctx - 1)
    def _():
        halo_copy(0, c + 1).start()

    def state_copy(g, way, peer, slot):
        return pltpu.make_async_remote_copy(
            src_ref=st_send.at[g, way],
            dst_ref=st_recv.at[g, slot],
            send_sem=st_ssem.at[g, peer],
            recv_sem=st_rsem.at[g, slot],
            device_id={"ctx": peer},
            device_id_type=MESH,
        )

    def edge_copy(g, part, target):
        streams = PARTS[part]
        return pltpu.make_async_remote_copy(
            src_ref=bsend.at[g, streams],
            dst_ref=brecv.at[g, streams],
            send_sem=b_ssem.at[part, g],
            recv_sem=b_rsem.at[part, g],
            device_id={"ctx": target},
            device_id_type=MESH,
        )

    def out_copy(g, part, peer, source):
        streams = PARTS[part]
        first = pl.multiple_of(source * chans + g * LANES, LANES)
        return pltpu.make_async_remote_copy(
            src_ref=send.at[g, streams, pl.ds(pl.multiple_of(peer * token_rows, token_rows), token_rows), :],
            dst_ref=sgrad.at[streams, :, pl.ds(first, LANES)],
            send_sem=out_ssem.at[part, g, peer],
            recv_sem=out_rsem.at[part, g, source],
            device_id={"ch": peer},
            device_id_type=MESH,
        )

    def own_copy(g):
        first = pl.multiple_of(h * chans + g * LANES, LANES)
        return pltpu.make_async_copy(
            send.at[g, :, pl.ds(pl.multiple_of(h * token_rows, token_rows), token_rows), :],
            sgrad.at[:, :, pl.ds(first, LANES)],
            own_sem.at[g],
        )

    sublane = lax.broadcasted_iota(jnp.int32, (ORDER, ROWS, LANES), 1)
    sublane_f = sublane.astype(f32)

    first_row = lax.broadcasted_iota(jnp.int32, (ROWS, LANES), 0) == 0
    last_row = lax.broadcasted_iota(jnp.int32, (ROWS, LANES), 0) == ROWS - 1

    def load_taps(slot):
        return [
            [jnp.broadcast_to(filt[slot, pl.ds(s * TAPS + p, 1), :], (ROWS, LANES)) for p in range(TAPS)]
            for s in range(3)
        ]

    def first_phase(g):
        slot = lax.rem(g, 2)
        base = h * (chans // GROUP_SIZE) + g * (LANES // GROUP_SIZE)
        window = base // LANES
        for s in range(3):
            all_taps[s * TAPS : (s + 1) * TAPS, :] = filt_ref[s, :, lanes(window)]
        of_lane = lax.broadcasted_iota(jnp.int32, (LANES, LANES), 1) // GROUP_SIZE + (base - window * LANES)
        pick = (lax.broadcasted_iota(jnp.int32, (LANES, LANES), 0) == of_lane).astype(f32)
        filt[slot] = jnp.dot(
            all_taps[...], pick, precision=lax.Precision.HIGHEST, preferred_element_type=f32
        )

        rate = rate_ref[:, lanes(g)]
        decay = spread(jnp.exp(-rate))
        taps = load_taps(slot)

        def forward(i, carry):
            state, one, two = carry
            now = [xf[s, pl.ds(STRIDE + i, ROWS, stride=STRIDE), :] for s in range(3)]
            q, k, v = [taps[s][0] * now[s] + taps[s][1] * one[s] + taps[s][2] * two[s] for s in range(3)]
            o = ogf[pl.ds(i, ROWS, stride=STRIDE), :]
            product = k * v
            qt[slot, i] = q
            kt[slot, i] = k
            vt[slot, i] = v
            ot[slot, i] = o
            pt[slot, i] = product
            at[slot, i] = o * q
            return (decay * state + product[None], tuple(now), one)

        zero = jnp.zeros((ORDER, ROWS, LANES), f32)
        one = tuple(xf[s, pl.ds(BLOCK - 1, ROWS, stride=STRIDE), :] for s in range(3))
        two = tuple(xf[s, pl.ds(BLOCK - 2, ROWS, stride=STRIDE), :] for s in range(3))
        state, _, _ = steps(forward, (zero, one, two))
        ef[slot] = state

        @pl.when(c > 0)
        def _():
            halo_copy(g, c).wait_recv()
            before = [halo[g, s].astype(f32) for s in range(3)]
            for i in range(TAPS - 1):
                more = []
                for s in range(3):
                    term = taps[s][i + 1] * jnp.broadcast_to(before[s][15:16], (ROWS, LANES))
                    if i == 0:
                        term = term + taps[s][2] * jnp.broadcast_to(before[s][14:15], (ROWS, LANES))
                    more.append(jnp.where(first_row, term, 0.0))
                q = qt[slot, i] + more[0]
                k = kt[slot, i] + more[1]
                v = vt[slot, i] + more[2]
                change = k * v - pt[slot, i]
                qt[slot, i] = q
                kt[slot, i] = k
                vt[slot, i] = v
                pt[slot, i] = k * v
                at[slot, i] = ot[slot, i] * q
                ef[slot] += spread(jnp.exp(-rate * float(BLOCK - 1 - i))) * change[None]

        wide = spread(rate) * (-float(BLOCK))
        st_send[g, 0] = jnp.sum(jnp.exp(wide * (ROWS - 1.0 - sublane_f)) * ef[slot], axis=1)

        def later(j, _):
            state_copy(g, 0, j, c).start()
            return 0

        lax.fori_loop(c + 1, nctx, later, 0)

        def back(i, state):
            return decay * state + at[slot, i][None]

        adj_state = steps(back, zero, True)
        eb[slot] = adj_state
        st_send[g, 1] = jnp.sum(jnp.exp(wide * sublane_f) * adj_state, axis=1)

        def earlier(j, _):
            state_copy(g, 1, j, c).start()
            return 0

        lax.fori_loop(0, c, earlier, 0)

    def second_phase(g):
        slot = lax.rem(g, 2)
        rate = rate_ref[:, lanes(g)]
        decay = spread(jnp.exp(-rate))
        amp = spread(res_ref[:, lanes(g)] * jnp.sqrt(2.0 * rate))
        taps = load_taps(slot)
        hop = jnp.exp(-rate * float(span))

        def arrive(j, total):
            state_copy(g, 0, j, j).wait_recv()
            return hop * total + st_recv[g, j]

        def arrive_back(k, total):
            j = nctx - 1 - k
            state_copy(g, 1, j, j).wait_recv()
            return hop * total + st_recv[g, j]

        none = jnp.zeros((ORDER, LANES), f32)
        def scan(emitted, entry, backward):
            def shift(a, by, fill):
                moved = pltpu.roll(a, ROWS - by if backward else by, 1)
                keep = sublane < ROWS - by if backward else sublane >= by
                return jnp.where(keep, moved, fill)

            total = shift(emitted, 1, spread(entry))
            factor = spread(jnp.exp(-rate * float(BLOCK)))
            for by in (1, 2, 4):
                total = total + factor * shift(total, by, 0.0)
                factor = factor * factor
            return total

        def short(s, i):
            nat[s, pl.ds(i, ROWS, stride=STRIDE), :] = (
                taps[s][0] * sg[s, i] + taps[s][1] * sg[s, i + 1] + taps[s][2] * sg[s, i + 2]
            )

        def narrow(s, first, last):
            def block(k, _):
                come = pl.ds(pl.multiple_of(k * STRIDE, 8), BLOCK)
                send[g, s, pl.ds(pl.multiple_of(k * BLOCK, BLOCK), BLOCK), :] = nat[s, come, :].astype(bf16)
                return 0

            lax.fori_loop(first, last, block, 0)

        early = nch * (ROWS - 1) // ROWS

        def finish_part(part):
            streams = PARTS[part]
            for s in range(streams.start, streams.start + streams.size):
                for r in range(TAPS - 1):
                    bsend[g, s, r] = sg[s, r]
                    sg[s, BLOCK + r] = pltpu.roll(sg[s, r], ROWS - 1, 0)

            @pl.when(c > 0)
            def _():
                edge_copy(g, part, c - 1).start()

            def some(i, _):
                for s in range(streams.start, streams.start + streams.size):
                    short(s, i)
                return 0

            steps(some, 0)
            for s in range(streams.start, streams.start + streams.size):
                narrow(s, 0, ROWS - 1)

            def go(k, _):
                peer = lax.rem(h + lax.rem(k + nch // 2 - 2, nch - 1) + 1, nch)

                @pl.when(peer < early)
                def _():
                    out_copy(g, part, peer, h).start()

                return 0

            lax.fori_loop(1, nch, go, 0)

        def forward(i, state):
            state = decay * state + pt[slot, i][None]
            long_out = jnp.sum(amp * state, axis=0)
            nat[3, pl.ds(i, ROWS, stride=STRIDE), :] = qt[slot, i] * long_out
            sg[0, i] = ot[slot, i] * long_out
            return state

        incoming = lax.fori_loop(0, c, arrive, none)
        steps(forward, scan(ef[slot], incoming, False))
        finish_part(0)

        def back(i, state):
            state = decay * state + at[slot, i][None]
            long_grad = jnp.sum(amp * state, axis=0)
            sg[1, i] = long_grad * vt[slot, i]
            sg[2, i] = long_grad * kt[slot, i]
            return state

        outgoing = lax.fori_loop(0, nctx - 1 - c, arrive_back, none)
        steps(back, scan(eb[slot], outgoing, True), True)
        finish_part(1)

        def narrow_lay(k, _):
            come = pl.ds(pl.multiple_of(k * STRIDE, 8), BLOCK)
            lay[pl.ds(pl.multiple_of(k * BLOCK, BLOCK), BLOCK), lanes(g)] = nat[3, come, :].astype(bf16)
            return 0

        lax.fori_loop(0, ROWS, narrow_lay, 0)

        @pl.when(c == nctx - 1)
        def _():
            brecv[g] = jnp.zeros((3, TAPS - 1, ROWS, LANES), f32)

        @pl.when(c < nctx - 1)
        def _():
            edge_copy(g, 0, c).wait_recv()
            edge_copy(g, 1, c).wait_recv()

        for s in range(3):
            for r in range(TAPS - 1):
                sg[s, BLOCK + r] = jnp.where(last_row, pltpu.roll(brecv[g, s, r], ROWS - 1, 0), sg[s, BLOCK + r])
            for i in range(BLOCK - TAPS + 1, BLOCK):
                short(s, i)
            narrow(s, ROWS - 1, ROWS)

        def rest(peer, _):
            @pl.when(peer != h)
            def _():
                out_copy(g, 0, peer, h).start()
                out_copy(g, 1, peer, h).start()

            return 0

        lax.fori_loop(early, nch, rest, 0)
        own_copy(g).start()

    def both(t, _):
        @pl.when(t < groups)
        def _():
            first_phase(t)

        @pl.when(t != 1)
        def _():
            second_phase(jnp.maximum(t - 1, 0))

        @pl.when(t + 1 < groups)
        def _():
            widen(t + 1)

            @pl.when(c < nctx - 1)
            def _():
                halo_copy(t + 1, c + 1).start()

        return 0

    lax.fori_loop(0, groups + 1, both, 0)

    def finish(g, _):
        @pl.when(c < nctx - 1)
        def _():
            halo_copy(g, c).wait_send()

        @pl.when(c > 0)
        def _():
            edge_copy(g, 0, c).wait_send()
            edge_copy(g, 1, c).wait_send()

        def later(j, _):
            state_copy(g, 0, j, c).wait_send()
            return 0

        def earlier(j, _):
            state_copy(g, 1, j, c).wait_send()
            return 0

        lax.fori_loop(c + 1, nctx, later, 0)
        lax.fori_loop(0, c, earlier, 0)
        own_copy(g).wait()

        def out(k, _):
            peer = lax.rem(h + k, nch)
            for part in range(2):
                out_copy(g, part, peer, h).wait_send()
                out_copy(g, part, peer, peer).wait_recv()
            return 0

        lax.fori_loop(1, nch, out, 0)
        return 0

    lax.fori_loop(0, groups, finish, 0)


def place(lay, sgrad, lay_out, sgrad_out, sem):
    rows, cut = lay.shape[0] // 4, sgrad.shape[2] // 4
    copies = []
    for k in range(4):
        part = pl.ds(k * cut, cut)
        for s in range(3):
            copies.append((sgrad.at[s, :, part], sgrad_out.at[s, :, part]))
        part = pl.ds(k * rows, rows)
        copies.append((lay.at[part], lay_out.at[part]))
    copies = [pltpu.make_async_copy(a, b, sem.at[n]) for n, (a, b) in enumerate(copies)]
    for copy in copies:
        copy.start()
    for copy in copies:
        copy.wait()


def shards(nctx, nch, streams_in, out_grad, decay_rate, residue, short_filter):
    _, span, chans = streams_in.shape
    assert span == ROWS * BLOCK and chans % LANES == 0
    groups = chans // LANES
    token_rows = span // nch
    rate = decay_rate.T
    res = residue.T
    filt = short_filter.transpose(0, 2, 1)
    turned = (2, BLOCK, ROWS, LANES)
    states = (2, ORDER, ROWS, LANES)
    edge = (groups, 3, TAPS - 1, ROWS, LANES)
    dma = pltpu.SemaphoreType.DMA
    whole = pl.BlockSpec(memory_space=pltpu.VMEM)
    held = pl.pallas_call(
        functools.partial(kernel, nctx, nch, groups),
        out_shape=(
            pltpu.VMEM((span, chans), bf16),
            pltpu.VMEM((3, token_rows, chans * nch), bf16),
        ),
        in_specs=[pl.BlockSpec(memory_space=pltpu.HBM)] * 2 + [whole] * 3,
        out_specs=(whole, whole),
        scratch_shapes=[
            pltpu.VMEM((groups, 3, span, LANES), bf16),
            pltpu.VMEM((groups, span, LANES), bf16),
            pltpu.VMEM((groups, 3, 16, LANES), bf16),
            pltpu.VMEM((3, (ROWS + 1) * STRIDE, LANES), f32),
            pltpu.VMEM((ROWS * STRIDE, LANES), f32),
            pltpu.VMEM((16, LANES), f32),
            pltpu.VMEM((2, 16, LANES), f32),
            *[pltpu.VMEM(turned, f32) for _ in range(6)],
            *[pltpu.VMEM(states, f32) for _ in range(2)],
            pltpu.VMEM((groups, 2, ORDER, LANES), f32),
            pltpu.VMEM((groups, nctx, ORDER, LANES), f32),
            pltpu.VMEM((3, BLOCK + TAPS - 1, ROWS, LANES), f32),
            pltpu.VMEM((4, ROWS * STRIDE, LANES), f32),
            pltpu.VMEM(edge, f32),
            pltpu.VMEM(edge, f32),
            pltpu.VMEM((groups, 3, span, LANES), bf16),
            dma((2, groups)),
            dma((groups,)),
            dma((groups,)),
            dma((groups, nctx)),
            dma((groups, nctx)),
            dma((2, groups)),
            dma((2, groups)),
            dma((2, groups, nch)),
            dma((2, groups, nch)),
            dma((groups,)),
        ],
        compiler_params=pltpu.CompilerParams(
            collective_id=0, has_side_effects=True, vmem_limit_bytes=48 * 1024 * 1024
        ),
        cost_estimate=pl.CostEstimate(
            flops=span * chans * 250, bytes_accessed=16 * span * chans, transcendentals=0
        ),
    )(streams_in, out_grad, rate, res, filt)
    return pl.pallas_call(
        place,
        out_shape=tuple(jax.ShapeDtypeStruct(a.shape, bf16) for a in held),
        in_specs=[pl.BlockSpec(memory_space=pl.ANY)] * 2,
        out_specs=(pl.BlockSpec(memory_space=pl.ANY),) * 2,
        scratch_shapes=[dma((16,))],
        compiler_params=pltpu.CompilerParams(vmem_limit_bytes=16 * 1024 * 1024),
    )(*held)


def solution(mesh):
    return jax.shard_map(
        functools.partial(shards, mesh.shape["ctx"], mesh.shape["ch"]),
        mesh=mesh,
        in_specs=(P(None, "ctx", "ch"), P("ctx", "ch"), P("ch", None), P("ch", None), P()),
        out_specs=(P("ctx", "ch"), P(None, ("ctx", "ch"), None)),
        check_vma=False,
    )
```

```python
import functools

import jax
import jax.numpy as jnp
from jax import lax
from jax.experimental import pallas as pl
from jax.experimental.pallas import tpu as pltpu
from jax.sharding import PartitionSpec as P

GROUP_SIZE = 16
TAPS = 3
BLOCK = 128
LANES = 128
ROWS = 8
ORDER = 16
STRIDE = 136
UNROLL = 8
MESH = pl.DeviceIdType.MESH
PARTS = (pl.ds(0, 1), pl.ds(1, 2))
f32 = jnp.float32
bf16 = jnp.bfloat16


def spread(rows):
    return jnp.broadcast_to(rows[:, None, :], (rows.shape[0], ROWS, LANES))


def steps(body, carry, backward=False, count=BLOCK):
    def some(j, carry):
        for u in range(UNROLL):
            i = j * UNROLL + u
            carry = body(count - 1 - i if backward else i, carry)
        return carry

    return lax.fori_loop(0, count // UNROLL, some, carry)


def kernel(
    nctx, nch, groups,
    x_hbm, og_hbm, rate_ref, res_ref, filt_ref,
    lay, sgrad,
    xin, ogin, halo, xf, ogf, all_taps, filt, qt, kt, vt, ot, pt, at, ef, eb,
    st_send, st_recv, sg, nat, bsend, brecv, send,
    in_sem, halo_send, halo_recv, st_ssem, st_rsem, b_ssem, b_rsem,
    out_ssem, out_rsem, own_sem,
):
    span = x_hbm.shape[1]
    chans = x_hbm.shape[2]
    token_rows = span // nch
    c = lax.axis_index("ctx")
    h = lax.axis_index("ch")

    def lanes(g):
        return pl.ds(pl.multiple_of(g * LANES, LANES), LANES)

    def x_copy(g):
        return pltpu.make_async_copy(x_hbm.at[:, :, lanes(g)], xin.at[g], in_sem.at[0, g])

    def og_copy(g):
        return pltpu.make_async_copy(og_hbm.at[:, lanes(g)], ogin.at[g], in_sem.at[1, g])

    def load(g, _):
        x_copy(g).start()
        og_copy(g).start()
        return 0

    load(0, 0)

    barrier = pltpu.get_barrier_semaphore()

    def greet_ch(k, _):
        pl.semaphore_signal(barrier, inc=1, device_id={"ch": lax.rem(h + k, nch)}, device_id_type=MESH)
        return 0

    def greet_ctx(k, _):
        pl.semaphore_signal(barrier, inc=1, device_id={"ctx": lax.rem(c + k, nctx)}, device_id_type=MESH)
        return 0

    lax.fori_loop(1, nctx, greet_ctx, 0)
    lax.fori_loop(1, nch, greet_ch, 0)

    all_taps[...] = jnp.zeros((16, LANES), f32)
    for s in range(3):
        xf[s, BLOCK - 16 : BLOCK, :] = jnp.zeros((16, LANES), f32)

    def widen(g):
        x_copy(g).wait()
        og_copy(g).wait()

        def block(k, _):
            come = pl.ds(pl.multiple_of(k * BLOCK, BLOCK), BLOCK)
            for s in range(3):
                xf[s, pl.ds(pl.multiple_of((k + 1) * STRIDE, 8), BLOCK), :] = xin[g, s, come, :].astype(f32)
            ogf[pl.ds(pl.multiple_of(k * STRIDE, 8), BLOCK), :] = ogin[g, come, :].astype(f32)
            return 0

        lax.fori_loop(0, ROWS, block, 0)

    widen(0)
    lax.fori_loop(1, groups, load, 0)
    pl.semaphore_wait(barrier, nch + nctx - 2)

    def halo_copy(g, target):
        return pltpu.make_async_remote_copy(
            src_ref=x_hbm.at[:, pl.ds(span - 16, 16), lanes(g)],
            dst_ref=halo.at[g],
            send_sem=halo_send.at[g],
            recv_sem=halo_recv.at[g],
            device_id={"ctx": target},
            device_id_type=MESH,
        )

    @pl.when(c < nctx - 1)
    def _():
        halo_copy(0, c + 1).start()

    def state_copy(g, way, peer, slot):
        return pltpu.make_async_remote_copy(
            src_ref=st_send.at[g, way],
            dst_ref=st_recv.at[g, slot],
            send_sem=st_ssem.at[g, peer],
            recv_sem=st_rsem.at[g, slot],
            device_id={"ctx": peer},
            device_id_type=MESH,
        )

    def edge_copy(g, part, target):
        streams = PARTS[part]
        return pltpu.make_async_remote_copy(
            src_ref=bsend.at[g, streams],
            dst_ref=brecv.at[g, streams],
            send_sem=b_ssem.at[part, g],
            recv_sem=b_rsem.at[part, g],
            device_id={"ctx": target},
            device_id_type=MESH,
        )

    def out_copy(g, part, peer, source):
        streams = PARTS[part]
        return pltpu.make_async_remote_copy(
            src_ref=send.at[g, streams, pl.ds(pl.multiple_of(peer * token_rows, token_rows), token_rows), :],
            dst_ref=sgrad.at[streams, source * groups + g],
            send_sem=out_ssem.at[part, g, peer],
            recv_sem=out_rsem.at[part, g, source],
            device_id={"ch": peer},
            device_id_type=MESH,
        )

    def own_copy(g):
        return pltpu.make_async_copy(
            send.at[g, :, pl.ds(pl.multiple_of(h * token_rows, token_rows), token_rows), :],
            sgrad.at[:, h * groups + g],
            own_sem.at[g],
        )

    sublane = lax.broadcasted_iota(jnp.int32, (ORDER, ROWS, LANES), 1)
    sublane_f = sublane.astype(f32)

    first_row = lax.broadcasted_iota(jnp.int32, (ROWS, LANES), 0) == 0
    last_row = lax.broadcasted_iota(jnp.int32, (ROWS, LANES), 0) == ROWS - 1

    def load_taps(slot):
        return [
            [jnp.broadcast_to(filt[slot, pl.ds(s * TAPS + p, 1), :], (ROWS, LANES)) for p in range(TAPS)]
            for s in range(3)
        ]

    def first_phase(g):
        slot = lax.rem(g, 2)
        base = h * (chans // GROUP_SIZE) + g * (LANES // GROUP_SIZE)
        window = base // LANES
        for s in range(3):
            all_taps[s * TAPS : (s + 1) * TAPS, :] = filt_ref[s, :, lanes(window)]
        of_lane = lax.broadcasted_iota(jnp.int32, (LANES, LANES), 1) // GROUP_SIZE + (base - window * LANES)
        pick = (lax.broadcasted_iota(jnp.int32, (LANES, LANES), 0) == of_lane).astype(f32)
        filt[slot] = jnp.dot(
            all_taps[...], pick, precision=lax.Precision.HIGHEST, preferred_element_type=f32
        )

        rate = rate_ref[:, lanes(g)]
        decay = spread(jnp.exp(-rate))
        taps = load_taps(slot)

        def forward(i, carry):
            state, one, two = carry
            now = [xf[s, pl.ds(STRIDE + i, ROWS, stride=STRIDE), :] for s in range(3)]
            q, k, v = [taps[s][0] * now[s] + taps[s][1] * one[s] + taps[s][2] * two[s] for s in range(3)]
            o = ogf[pl.ds(i, ROWS, stride=STRIDE), :]
            product = k * v
            qt[slot, i] = q
            kt[slot, i] = k
            vt[slot, i] = v
            ot[slot, i] = o
            pt[slot, i] = product
            at[slot, i] = o * q
            return (decay * state + product[None], tuple(now), one)

        zero = jnp.zeros((ORDER, ROWS, LANES), f32)
        one = tuple(xf[s, pl.ds(BLOCK - 1, ROWS, stride=STRIDE), :] for s in range(3))
        two = tuple(xf[s, pl.ds(BLOCK - 2, ROWS, stride=STRIDE), :] for s in range(3))
        state, _, _ = steps(forward, (zero, one, two))
        ef[slot] = state

        @pl.when(c > 0)
        def _():
            halo_copy(g, c).wait_recv()
            before = [halo[g, s].astype(f32) for s in range(3)]
            for i in range(TAPS - 1):
                more = []
                for s in range(3):
                    term = taps[s][i + 1] * jnp.broadcast_to(before[s][15:16], (ROWS, LANES))
                    if i == 0:
                        term = term + taps[s][2] * jnp.broadcast_to(before[s][14:15], (ROWS, LANES))
                    more.append(jnp.where(first_row, term, 0.0))
                q = qt[slot, i] + more[0]
                k = kt[slot, i] + more[1]
                v = vt[slot, i] + more[2]
                change = k * v - pt[slot, i]
                qt[slot, i] = q
                kt[slot, i] = k
                vt[slot, i] = v
                pt[slot, i] = k * v
                at[slot, i] = ot[slot, i] * q
                ef[slot] += spread(jnp.exp(-rate * float(BLOCK - 1 - i))) * change[None]

        wide = spread(rate) * (-float(BLOCK))
        st_send[g, 0] = jnp.sum(jnp.exp(wide * (ROWS - 1.0 - sublane_f)) * ef[slot], axis=1)

        def later(j, _):
            state_copy(g, 0, j, c).start()
            return 0

        lax.fori_loop(c + 1, nctx, later, 0)

        def back(i, state):
            return decay * state + at[slot, i][None]

        adj_state = steps(back, zero, True)
        eb[slot] = adj_state
        st_send[g, 1] = jnp.sum(jnp.exp(wide * sublane_f) * adj_state, axis=1)

        def earlier(j, _):
            state_copy(g, 1, j, c).start()
            return 0

        lax.fori_loop(0, c, earlier, 0)

    def second_phase(g):
        slot = lax.rem(g, 2)
        rate = rate_ref[:, lanes(g)]
        decay = spread(jnp.exp(-rate))
        amp = spread(res_ref[:, lanes(g)] * jnp.sqrt(2.0 * rate))
        taps = load_taps(slot)
        hop = jnp.exp(-rate * float(span))

        def arrive(j, total):
            state_copy(g, 0, j, j).wait_recv()
            return hop * total + st_recv[g, j]

        def arrive_back(k, total):
            j = nctx - 1 - k
            state_copy(g, 1, j, j).wait_recv()
            return hop * total + st_recv[g, j]

        none = jnp.zeros((ORDER, LANES), f32)
        def scan(emitted, entry, backward):
            def shift(a, by, fill):
                moved = pltpu.roll(a, ROWS - by if backward else by, 1)
                keep = sublane < ROWS - by if backward else sublane >= by
                return jnp.where(keep, moved, fill)

            total = shift(emitted, 1, spread(entry))
            factor = spread(jnp.exp(-rate * float(BLOCK)))
            for by in (1, 2, 4):
                total = total + factor * shift(total, by, 0.0)
                factor = factor * factor
            return total

        def short(s, i):
            nat[s, pl.ds(i, ROWS, stride=STRIDE), :] = (
                taps[s][0] * sg[s, i] + taps[s][1] * sg[s, i + 1] + taps[s][2] * sg[s, i + 2]
            )

        def narrow(s, first, last):
            def block(k, _):
                come = pl.ds(pl.multiple_of(k * STRIDE, 8), BLOCK)
                send[g, s, pl.ds(pl.multiple_of(k * BLOCK, BLOCK), BLOCK), :] = nat[s, come, :].astype(bf16)
                return 0

            lax.fori_loop(first, last, block, 0)

        early = nch * (ROWS - 1) // ROWS

        def finish_part(part):
            streams = PARTS[part]
            for s in range(streams.start, streams.start + streams.size):
                for r in range(TAPS - 1):
                    bsend[g, s, r] = sg[s, r]
                    sg[s, BLOCK + r] = pltpu.roll(sg[s, r], ROWS - 1, 0)

            @pl.when(c > 0)
            def _():
                edge_copy(g, part, c - 1).start()

            def some(i, _):
                for s in range(streams.start, streams.start + streams.size):
                    short(s, i)
                return 0

            steps(some, 0)
            for s in range(streams.start, streams.start + streams.size):
                narrow(s, 0, ROWS - 1)

            def go(k, _):
                peer = lax.rem(h + lax.rem(k + nch // 2 - 2, nch - 1) + 1, nch)

                @pl.when(peer < early)
                def _():
                    out_copy(g, part, peer, h).start()

                return 0

            lax.fori_loop(1, nch, go, 0)

        def forward(i, state):
            state = decay * state + pt[slot, i][None]
            long_out = jnp.sum(amp * state, axis=0)
            nat[3, pl.ds(i, ROWS, stride=STRIDE), :] = qt[slot, i] * long_out
            sg[0, i] = ot[slot, i] * long_out
            return state

        incoming = lax.fori_loop(0, c, arrive, none)
        steps(forward, scan(ef[slot], incoming, False))
        finish_part(0)

        def back(i, state):
            state = decay * state + at[slot, i][None]
            long_grad = jnp.sum(amp * state, axis=0)
            sg[1, i] = long_grad * vt[slot, i]
            sg[2, i] = long_grad * kt[slot, i]
            return state

        outgoing = lax.fori_loop(0, nctx - 1 - c, arrive_back, none)
        steps(back, scan(eb[slot], outgoing, True), True)
        finish_part(1)

        def narrow_lay(k, _):
            come = pl.ds(pl.multiple_of(k * STRIDE, 8), BLOCK)
            lay[pl.ds(pl.multiple_of(k * BLOCK, BLOCK), BLOCK), lanes(g)] = nat[3, come, :].astype(bf16)
            return 0

        lax.fori_loop(0, ROWS, narrow_lay, 0)

        @pl.when(c == nctx - 1)
        def _():
            brecv[g] = jnp.zeros((3, TAPS - 1, ROWS, LANES), f32)

        @pl.when(c < nctx - 1)
        def _():
            edge_copy(g, 0, c).wait_recv()
            edge_copy(g, 1, c).wait_recv()

        for s in range(3):
            for r in range(TAPS - 1):
                sg[s, BLOCK + r] = jnp.where(last_row, pltpu.roll(brecv[g, s, r], ROWS - 1, 0), sg[s, BLOCK + r])
            for i in range(BLOCK - TAPS + 1, BLOCK):
                short(s, i)
            narrow(s, ROWS - 1, ROWS)

        def rest(peer, _):
            @pl.when(peer != h)
            def _():
                out_copy(g, 0, peer, h).start()
                out_copy(g, 1, peer, h).start()

            return 0

        lax.fori_loop(early, nch, rest, 0)
        own_copy(g).start()

    def both(t, _):
        @pl.when(t < groups)
        def _():
            first_phase(t)

        @pl.when(t != 1)
        def _():
            second_phase(jnp.maximum(t - 1, 0))

        @pl.when(t + 1 < groups)
        def _():
            widen(t + 1)

            @pl.when(c < nctx - 1)
            def _():
                halo_copy(t + 1, c + 1).start()

        return 0

    lax.fori_loop(0, groups + 1, both, 0)

    def finish(g, _):
        @pl.when(c < nctx - 1)
        def _():
            halo_copy(g, c).wait_send()

        @pl.when(c > 0)
        def _():
            edge_copy(g, 0, c).wait_send()
            edge_copy(g, 1, c).wait_send()

        def later(j, _):
            state_copy(g, 0, j, c).wait_send()
            return 0

        def earlier(j, _):
            state_copy(g, 1, j, c).wait_send()
            return 0

        lax.fori_loop(c + 1, nctx, later, 0)
        lax.fori_loop(0, c, earlier, 0)
        own_copy(g).wait()

        def out(k, _):
            peer = lax.rem(h + k, nch)
            for part in range(2):
                out_copy(g, part, peer, h).wait_send()
                out_copy(g, part, peer, peer).wait_recv()
            return 0

        lax.fori_loop(1, nch, out, 0)
        return 0

    lax.fori_loop(0, groups, finish, 0)


def place(lay, sgrad, lay_out, sgrad_out, sem):
    slots = sgrad.shape[1]

    def part(j):
        to = pl.ds(pl.multiple_of(j * LANES, LANES), LANES)
        return pltpu.make_async_copy(sgrad.at[:, j], sgrad_out.at[:, :, to], sem.at[j])

    def start(j, _):
        part(j).start()
        return 0

    def finish(j, _):
        part(j).wait()
        return 0

    lax.fori_loop(0, slots, start, 0)
    whole = pltpu.make_async_copy(lay, lay_out, sem.at[slots])
    whole.start()
    lax.fori_loop(0, slots, finish, 0)
    whole.wait()


def shards(nctx, nch, streams_in, out_grad, decay_rate, residue, short_filter):
    _, span, chans = streams_in.shape
    assert span == ROWS * BLOCK and chans % LANES == 0
    groups = chans // LANES
    token_rows = span // nch
    rate = decay_rate.T
    res = residue.T
    filt = short_filter.transpose(0, 2, 1)
    turned = (2, BLOCK, ROWS, LANES)
    states = (2, ORDER, ROWS, LANES)
    edge = (groups, 3, TAPS - 1, ROWS, LANES)
    dma = pltpu.SemaphoreType.DMA
    whole = pl.BlockSpec(memory_space=pltpu.VMEM)
    held = pl.pallas_call(
        functools.partial(kernel, nctx, nch, groups),
        out_shape=(
            pltpu.VMEM((span, chans), bf16),
            pltpu.VMEM((3, nch * groups, token_rows, LANES), bf16),
        ),
        in_specs=[pl.BlockSpec(memory_space=pltpu.HBM)] * 2 + [whole] * 3,
        out_specs=(whole, whole),
        scratch_shapes=[
            pltpu.VMEM((groups, 3, span, LANES), bf16),
            pltpu.VMEM((groups, span, LANES), bf16),
            pltpu.VMEM((groups, 3, 16, LANES), bf16),
            pltpu.VMEM((3, (ROWS + 1) * STRIDE, LANES), f32),
            pltpu.VMEM((ROWS * STRIDE, LANES), f32),
            pltpu.VMEM((16, LANES), f32),
            pltpu.VMEM((2, 16, LANES), f32),
            *[pltpu.VMEM(turned, f32) for _ in range(6)],
            *[pltpu.VMEM(states, f32) for _ in range(2)],
            pltpu.VMEM((groups, 2, ORDER, LANES), f32),
            pltpu.VMEM((groups, nctx, ORDER, LANES), f32),
            pltpu.VMEM((3, BLOCK + TAPS - 1, ROWS, LANES), f32),
            pltpu.VMEM((4, ROWS * STRIDE, LANES), f32),
            pltpu.VMEM(edge, f32),
            pltpu.VMEM(edge, f32),
            pltpu.VMEM((groups, 3, span, LANES), bf16),
            dma((2, groups)),
            dma((groups,)),
            dma((groups,)),
            dma((groups, nctx)),
            dma((groups, nctx)),
            dma((2, groups)),
            dma((2, groups)),
            dma((2, groups, nch)),
            dma((2, groups, nch)),
            dma((groups,)),
        ],
        compiler_params=pltpu.CompilerParams(
            collective_id=0, has_side_effects=True, vmem_limit_bytes=48 * 1024 * 1024
        ),
        cost_estimate=pl.CostEstimate(
            flops=span * chans * 250, bytes_accessed=16 * span * chans, transcendentals=0
        ),
    )(streams_in, out_grad, rate, res, filt)
    return pl.pallas_call(
        place,
        out_shape=(
            jax.ShapeDtypeStruct((span, chans), bf16),
            jax.ShapeDtypeStruct((3, token_rows, chans * nch), bf16),
        ),
        in_specs=[pl.BlockSpec(memory_space=pl.ANY)] * 2,
        out_specs=(pl.BlockSpec(memory_space=pl.ANY),) * 2,
        scratch_shapes=[dma((nch * groups + 1,))],
        compiler_params=pltpu.CompilerParams(vmem_limit_bytes=16 * 1024 * 1024),
    )(*held)


def solution(mesh):
    return jax.shard_map(
        functools.partial(shards, mesh.shape["ctx"], mesh.shape["ch"]),
        mesh=mesh,
        in_specs=(P(None, "ctx", "ch"), P("ctx", "ch"), P("ch", None), P("ch", None), P()),
        out_specs=(P("ctx", "ch"), P(None, ("ctx", "ch"), None)),
        check_vma=False,
    )
```

```python
import functools

import jax
import jax.numpy as jnp
from jax import lax
from jax.experimental import pallas as pl
from jax.experimental.pallas import tpu as pltpu
from jax.sharding import PartitionSpec as P

GROUP_SIZE = 16
TAPS = 3
BLOCK = 128
LANES = 128
ROWS = 8
ORDER = 16
STRIDE = 136
UNROLL = 8
MESH = pl.DeviceIdType.MESH
PARTS = (pl.ds(0, 1), pl.ds(1, 2))
f32 = jnp.float32
bf16 = jnp.bfloat16


def spread(rows):
    return jnp.broadcast_to(rows[:, None, :], (rows.shape[0], ROWS, LANES))


def steps(body, carry, backward=False, count=BLOCK):
    def some(j, carry):
        for u in range(UNROLL):
            i = j * UNROLL + u
            carry = body(count - 1 - i if backward else i, carry)
        return carry

    return lax.fori_loop(0, count // UNROLL, some, carry)


def kernel(
    nctx, nch, groups,
    x_hbm, og_hbm, rate_ref, res_ref, filt_ref,
    lay, sgrad,
    xin, ogin, halo, xf, ogf, all_taps, filt, qt, kt, vt, ot, pt, at, ef, eb,
    st_send, st_recv, sg, nat, bsend, brecv, send,
    in_sem, halo_send, halo_recv, st_ssem, st_rsem, b_ssem, b_rsem,
    out_ssem, out_rsem, own_sem,
):
    span = x_hbm.shape[1]
    chans = x_hbm.shape[2]
    token_rows = span // nch
    c = lax.axis_index("ctx")
    h = lax.axis_index("ch")

    def lanes(g):
        return pl.ds(pl.multiple_of(g * LANES, LANES), LANES)

    def x_copy(g):
        return pltpu.make_async_copy(x_hbm.at[:, :, lanes(g)], xin.at[g], in_sem.at[0, g])

    def og_copy(g):
        return pltpu.make_async_copy(og_hbm.at[:, lanes(g)], ogin.at[g], in_sem.at[1, g])

    def load(g, _):
        x_copy(g).start()
        og_copy(g).start()
        return 0

    load(0, 0)

    barrier = pltpu.get_barrier_semaphore()

    def greet_ch(k, _):
        pl.semaphore_signal(barrier, inc=1, device_id={"ch": lax.rem(h + k, nch)}, device_id_type=MESH)
        return 0

    def greet_ctx(k, _):
        pl.semaphore_signal(barrier, inc=1, device_id={"ctx": lax.rem(c + k, nctx)}, device_id_type=MESH)
        return 0

    lax.fori_loop(1, nctx, greet_ctx, 0)
    lax.fori_loop(1, nch, greet_ch, 0)

    all_taps[...] = jnp.zeros((16, LANES), f32)
    for s in range(3):
        xf[s, BLOCK - 16 : BLOCK, :] = jnp.zeros((16, LANES), f32)

    def widen(g):
        x_copy(g).wait()
        og_copy(g).wait()

        def block(k, _):
            come = pl.ds(pl.multiple_of(k * BLOCK, BLOCK), BLOCK)
            for s in range(3):
                xf[s, pl.ds(pl.multiple_of((k + 1) * STRIDE, 8), BLOCK), :] = xin[g, s, come, :].astype(f32)
            ogf[pl.ds(pl.multiple_of(k * STRIDE, 8), BLOCK), :] = ogin[g, come, :].astype(f32)
            return 0

        lax.fori_loop(0, ROWS, block, 0)

    widen(0)
    lax.fori_loop(1, groups, load, 0)
    pl.semaphore_wait(barrier, nch + nctx - 2)

    def halo_copy(g, target):
        return pltpu.make_async_remote_copy(
            src_ref=x_hbm.at[:, pl.ds(span - 16, 16), lanes(g)],
            dst_ref=halo.at[g],
            send_sem=halo_send.at[g],
            recv_sem=halo_recv.at[g],
            device_id={"ctx": target},
            device_id_type=MESH,
        )

    @pl.when(c < nctx - 1)
    def _():
        halo_copy(0, c + 1).start()

    def state_copy(g, way, peer, slot):
        return pltpu.make_async_remote_copy(
            src_ref=st_send.at[g, way],
            dst_ref=st_recv.at[g, slot],
            send_sem=st_ssem.at[g, peer],
            recv_sem=st_rsem.at[g, slot],
            device_id={"ctx": peer},
            device_id_type=MESH,
        )

    def edge_copy(g, part, target):
        streams = PARTS[part]
        return pltpu.make_async_remote_copy(
            src_ref=bsend.at[g, streams],
            dst_ref=brecv.at[g, streams],
            send_sem=b_ssem.at[part, g],
            recv_sem=b_rsem.at[part, g],
            device_id={"ctx": target},
            device_id_type=MESH,
        )

    def out_copy(g, part, peer, source):
        streams = PARTS[part]
        first = pl.multiple_of(source * chans + g * LANES, LANES)
        return pltpu.make_async_remote_copy(
            src_ref=send.at[g, streams, pl.ds(pl.multiple_of(peer * token_rows, token_rows), token_rows), :],
            dst_ref=sgrad.at[streams, :, pl.ds(first, LANES)],
            send_sem=out_ssem.at[part, g, peer],
            recv_sem=out_rsem.at[part, g, source],
            device_id={"ch": peer},
            device_id_type=MESH,
        )

    def own_copy(g):
        first = pl.multiple_of(h * chans + g * LANES, LANES)
        return pltpu.make_async_copy(
            send.at[g, :, pl.ds(pl.multiple_of(h * token_rows, token_rows), token_rows), :],
            sgrad.at[:, :, pl.ds(first, LANES)],
            own_sem.at[g],
        )

    sublane = lax.broadcasted_iota(jnp.int32, (ORDER, ROWS, LANES), 1)
    sublane_f = sublane.astype(f32)

    first_row = lax.broadcasted_iota(jnp.int32, (ROWS, LANES), 0) == 0
    last_row = lax.broadcasted_iota(jnp.int32, (ROWS, LANES), 0) == ROWS - 1

    def load_taps(slot):
        return [
            [jnp.broadcast_to(filt[slot, pl.ds(s * TAPS + p, 1), :], (ROWS, LANES)) for p in range(TAPS)]
            for s in range(3)
        ]

    def first_phase(g):
        slot = lax.rem(g, 2)
        base = h * (chans // GROUP_SIZE) + g * (LANES // GROUP_SIZE)
        window = base // LANES
        for s in range(3):
            all_taps[s * TAPS : (s + 1) * TAPS, :] = filt_ref[s, :, lanes(window)]
        of_lane = lax.broadcasted_iota(jnp.int32, (LANES, LANES), 1) // GROUP_SIZE + (base - window * LANES)
        pick = (lax.broadcasted_iota(jnp.int32, (LANES, LANES), 0) == of_lane).astype(f32)
        filt[slot] = jnp.dot(
            all_taps[...], pick, precision=lax.Precision.HIGHEST, preferred_element_type=f32
        )

        rate = rate_ref[:, lanes(g)]
        decay = spread(jnp.exp(-rate))
        taps = load_taps(slot)

        def forward(i, carry):
            state, one, two = carry
            now = [xf[s, pl.ds(STRIDE + i, ROWS, stride=STRIDE), :] for s in range(3)]
            q, k, v = [taps[s][0] * now[s] + taps[s][1] * one[s] + taps[s][2] * two[s] for s in range(3)]
            o = ogf[pl.ds(i, ROWS, stride=STRIDE), :]
            product = k * v
            qt[slot, i] = q
            kt[slot, i] = k
            vt[slot, i] = v
            ot[slot, i] = o
            pt[slot, i] = product
            at[slot, i] = o * q
            return (decay * state + product[None], tuple(now), one)

        zero = jnp.zeros((ORDER, ROWS, LANES), f32)
        one = tuple(xf[s, pl.ds(BLOCK - 1, ROWS, stride=STRIDE), :] for s in range(3))
        two = tuple(xf[s, pl.ds(BLOCK - 2, ROWS, stride=STRIDE), :] for s in range(3))
        state, _, _ = steps(forward, (zero, one, two))
        ef[slot] = state

        @pl.when(c > 0)
        def _():
            halo_copy(g, c).wait_recv()
            before = [halo[g, s].astype(f32) for s in range(3)]
            for i in range(TAPS - 1):
                more = []
                for s in range(3):
                    term = taps[s][i + 1] * jnp.broadcast_to(before[s][15:16], (ROWS, LANES))
                    if i == 0:
                        term = term + taps[s][2] * jnp.broadcast_to(before[s][14:15], (ROWS, LANES))
                    more.append(jnp.where(first_row, term, 0.0))
                q = qt[slot, i] + more[0]
                k = kt[slot, i] + more[1]
                v = vt[slot, i] + more[2]
                change = k * v - pt[slot, i]
                qt[slot, i] = q
                kt[slot, i] = k
                vt[slot, i] = v
                pt[slot, i] = k * v
                at[slot, i] = ot[slot, i] * q
                ef[slot] += spread(jnp.exp(-rate * float(BLOCK - 1 - i))) * change[None]

        wide = spread(rate) * (-float(BLOCK))
        st_send[g, 0] = jnp.sum(jnp.exp(wide * (ROWS - 1.0 - sublane_f)) * ef[slot], axis=1)

        def later(j, _):
            state_copy(g, 0, j, c).start()
            return 0

        lax.fori_loop(c + 1, nctx, later, 0)

        def back(i, state):
            return decay * state + at[slot, i][None]

        adj_state = steps(back, zero, True)
        eb[slot] = adj_state
        st_send[g, 1] = jnp.sum(jnp.exp(wide * sublane_f) * adj_state, axis=1)

        def earlier(j, _):
            state_copy(g, 1, j, c).start()
            return 0

        lax.fori_loop(0, c, earlier, 0)

    def second_phase(g):
        slot = lax.rem(g, 2)
        rate = rate_ref[:, lanes(g)]
        decay = spread(jnp.exp(-rate))
        amp = spread(res_ref[:, lanes(g)] * jnp.sqrt(2.0 * rate))
        taps = load_taps(slot)
        hop = jnp.exp(-rate * float(span))

        def arrive(j, total):
            state_copy(g, 0, j, j).wait_recv()
            return hop * total + st_recv[g, j]

        def arrive_back(k, total):
            j = nctx - 1 - k
            state_copy(g, 1, j, j).wait_recv()
            return hop * total + st_recv[g, j]

        none = jnp.zeros((ORDER, LANES), f32)
        def scan(emitted, entry, backward):
            def shift(a, by, fill):
                moved = pltpu.roll(a, ROWS - by if backward else by, 1)
                keep = sublane < ROWS - by if backward else sublane >= by
                return jnp.where(keep, moved, fill)

            total = shift(emitted, 1, spread(entry))
            factor = spread(jnp.exp(-rate * float(BLOCK)))
            for by in (1, 2, 4):
                total = total + factor * shift(total, by, 0.0)
                factor = factor * factor
            return total

        def short(s, i):
            nat[s, pl.ds(i, ROWS, stride=STRIDE), :] = (
                taps[s][0] * sg[s, i] + taps[s][1] * sg[s, i + 1] + taps[s][2] * sg[s, i + 2]
            )

        def narrow(s, first, last):
            def block(k, _):
                come = pl.ds(pl.multiple_of(k * STRIDE, 8), BLOCK)
                send[g, s, pl.ds(pl.multiple_of(k * BLOCK, BLOCK), BLOCK), :] = nat[s, come, :].astype(bf16)
                return 0

            lax.fori_loop(first, last, block, 0)

        early = nch * (ROWS - 1) // ROWS

        def finish_part(part):
            streams = PARTS[part]
            for s in range(streams.start, streams.start + streams.size):
                for r in range(TAPS - 1):
                    bsend[g, s, r] = sg[s, r]
                    sg[s, BLOCK + r] = pltpu.roll(sg[s, r], ROWS - 1, 0)

            @pl.when(c > 0)
            def _():
                edge_copy(g, part, c - 1).start()

            def some(i, _):
                for s in range(streams.start, streams.start + streams.size):
                    short(s, i)
                return 0

            steps(some, 0)
            for s in range(streams.start, streams.start + streams.size):
                narrow(s, 0, ROWS - 1)

            def go(k, _):
                peer, low, high = 0, 1, nch // 2
                while high > 0:
                    flip, mine = lax.rem(lax.div(k, low), 2), lax.rem(lax.div(h, high), 2)
                    peer = peer + high * (flip + mine - 2 * flip * mine)
                    low, high = low * 2, high // 2

                @pl.when(peer < early)
                def _():
                    out_copy(g, part, peer, h).start()

                return 0

            lax.fori_loop(1, nch, go, 0)

        def forward(i, state):
            state = decay * state + pt[slot, i][None]
            long_out = jnp.sum(amp * state, axis=0)
            nat[3, pl.ds(i, ROWS, stride=STRIDE), :] = qt[slot, i] * long_out
            sg[0, i] = ot[slot, i] * long_out
            return state

        incoming = lax.fori_loop(0, c, arrive, none)
        steps(forward, scan(ef[slot], incoming, False))
        finish_part(0)

        def back(i, state):
            state = decay * state + at[slot, i][None]
            long_grad = jnp.sum(amp * state, axis=0)
            sg[1, i] = long_grad * vt[slot, i]
            sg[2, i] = long_grad * kt[slot, i]
            return state

        outgoing = lax.fori_loop(0, nctx - 1 - c, arrive_back, none)
        steps(back, scan(eb[slot], outgoing, True), True)
        finish_part(1)

        def narrow_lay(k, _):
            come = pl.ds(pl.multiple_of(k * STRIDE, 8), BLOCK)
            lay[pl.ds(pl.multiple_of(k * BLOCK, BLOCK), BLOCK), lanes(g)] = nat[3, come, :].astype(bf16)
            return 0

        lax.fori_loop(0, ROWS, narrow_lay, 0)

        @pl.when(c == nctx - 1)
        def _():
            brecv[g] = jnp.zeros((3, TAPS - 1, ROWS, LANES), f32)

        @pl.when(c < nctx - 1)
        def _():
            edge_copy(g, 0, c).wait_recv()
            edge_copy(g, 1, c).wait_recv()

        for s in range(3):
            for r in range(TAPS - 1):
                sg[s, BLOCK + r] = jnp.where(last_row, pltpu.roll(brecv[g, s, r], ROWS - 1, 0), sg[s, BLOCK + r])
            for i in range(BLOCK - TAPS + 1, BLOCK):
                short(s, i)
            narrow(s, ROWS - 1, ROWS)

        def rest(peer, _):
            @pl.when(peer != h)
            def _():
                out_copy(g, 0, peer, h).start()
                out_copy(g, 1, peer, h).start()

            return 0

        lax.fori_loop(early, nch, rest, 0)
        own_copy(g).start()

    def both(t, _):
        @pl.when(t < groups)
        def _():
            first_phase(t)

        @pl.when(t != 1)
        def _():
            second_phase(jnp.maximum(t - 1, 0))

        @pl.when(t + 1 < groups)
        def _():
            widen(t + 1)

            @pl.when(c < nctx - 1)
            def _():
                halo_copy(t + 1, c + 1).start()

        return 0

    lax.fori_loop(0, groups + 1, both, 0)

    def finish(g, _):
        @pl.when(c < nctx - 1)
        def _():
            halo_copy(g, c).wait_send()

        @pl.when(c > 0)
        def _():
            edge_copy(g, 0, c).wait_send()
            edge_copy(g, 1, c).wait_send()

        def later(j, _):
            state_copy(g, 0, j, c).wait_send()
            return 0

        def earlier(j, _):
            state_copy(g, 1, j, c).wait_send()
            return 0

        lax.fori_loop(c + 1, nctx, later, 0)
        lax.fori_loop(0, c, earlier, 0)
        own_copy(g).wait()

        def out(k, _):
            peer = lax.rem(h + k, nch)
            for part in range(2):
                out_copy(g, part, peer, h).wait_send()
                out_copy(g, part, peer, peer).wait_recv()
            return 0

        lax.fori_loop(1, nch, out, 0)
        return 0

    lax.fori_loop(0, groups, finish, 0)


def place(lay, sgrad, lay_out, sgrad_out, sem):
    rows, cut = lay.shape[0] // 4, sgrad.shape[2] // 4
    copies = []
    for k in range(4):
        part = pl.ds(k * cut, cut)
        for s in range(3):
            copies.append((sgrad.at[s, :, part], sgrad_out.at[s, :, part]))
        part = pl.ds(k * rows, rows)
        copies.append((lay.at[part], lay_out.at[part]))
    copies = [pltpu.make_async_copy(a, b, sem.at[n]) for n, (a, b) in enumerate(copies)]
    for copy in copies:
        copy.start()
    for copy in copies:
        copy.wait()


def shards(nctx, nch, streams_in, out_grad, decay_rate, residue, short_filter):
    _, span, chans = streams_in.shape
    assert span == ROWS * BLOCK and chans % LANES == 0
    groups = chans // LANES
    token_rows = span // nch
    rate = decay_rate.T
    res = residue.T
    filt = short_filter.transpose(0, 2, 1)
    turned = (2, BLOCK, ROWS, LANES)
    states = (2, ORDER, ROWS, LANES)
    edge = (groups, 3, TAPS - 1, ROWS, LANES)
    dma = pltpu.SemaphoreType.DMA
    whole = pl.BlockSpec(memory_space=pltpu.VMEM)
    held = pl.pallas_call(
        functools.partial(kernel, nctx, nch, groups),
        out_shape=(
            pltpu.VMEM((span, chans), bf16),
            pltpu.VMEM((3, token_rows, chans * nch), bf16),
        ),
        in_specs=[pl.BlockSpec(memory_space=pltpu.HBM)] * 2 + [whole] * 3,
        out_specs=(whole, whole),
        scratch_shapes=[
            pltpu.VMEM((groups, 3, span, LANES), bf16),
            pltpu.VMEM((groups, span, LANES), bf16),
            pltpu.VMEM((groups, 3, 16, LANES), bf16),
            pltpu.VMEM((3, (ROWS + 1) * STRIDE, LANES), f32),
            pltpu.VMEM((ROWS * STRIDE, LANES), f32),
            pltpu.VMEM((16, LANES), f32),
            pltpu.VMEM((2, 16, LANES), f32),
            *[pltpu.VMEM(turned, f32) for _ in range(6)],
            *[pltpu.VMEM(states, f32) for _ in range(2)],
            pltpu.VMEM((groups, 2, ORDER, LANES), f32),
            pltpu.VMEM((groups, nctx, ORDER, LANES), f32),
            pltpu.VMEM((3, BLOCK + TAPS - 1, ROWS, LANES), f32),
            pltpu.VMEM((4, ROWS * STRIDE, LANES), f32),
            pltpu.VMEM(edge, f32),
            pltpu.VMEM(edge, f32),
            pltpu.VMEM((groups, 3, span, LANES), bf16),
            dma((2, groups)),
            dma((groups,)),
            dma((groups,)),
            dma((groups, nctx)),
            dma((groups, nctx)),
            dma((2, groups)),
            dma((2, groups)),
            dma((2, groups, nch)),
            dma((2, groups, nch)),
            dma((groups,)),
        ],
        compiler_params=pltpu.CompilerParams(
            collective_id=0, has_side_effects=True, vmem_limit_bytes=48 * 1024 * 1024
        ),
        cost_estimate=pl.CostEstimate(
            flops=span * chans * 250, bytes_accessed=16 * span * chans, transcendentals=0
        ),
    )(streams_in, out_grad, rate, res, filt)
    return pl.pallas_call(
        place,
        out_shape=tuple(jax.ShapeDtypeStruct(a.shape, bf16) for a in held),
        in_specs=[pl.BlockSpec(memory_space=pl.ANY)] * 2,
        out_specs=(pl.BlockSpec(memory_space=pl.ANY),) * 2,
        scratch_shapes=[dma((16,))],
        compiler_params=pltpu.CompilerParams(vmem_limit_bytes=16 * 1024 * 1024),
    )(*held)


def solution(mesh):
    return jax.shard_map(
        functools.partial(shards, mesh.shape["ctx"], mesh.shape["ch"]),
        mesh=mesh,
        in_specs=(P(None, "ctx", "ch"), P("ctx", "ch"), P("ch", None), P("ch", None), P()),
        out_specs=(P("ctx", "ch"), P(None, ("ctx", "ch"), None)),
        check_vma=False,
    )
```
